32 devices in a mesh: dp: 16 (over z, y, x), fsdp: 2 (over core).
Axes of the slice: x: 2, y: 2, z: 4, core: 2. Of those that a mesh axis runs over, the one named last changes fastest.
Arguments:
- query_emb: bfloat16 [8192, 4096], P('dp', 'fsdp')
- passage_emb: bfloat16 [16384, 4096], P('dp', 'fsdp')
- cand_blocks: int32 [64, 4], P('dp'), may hold values from 0 to 127, as said below
- positive: int32 [8192], P('dp'), may hold values from 0 to 511
Outputs:
- losses: float32 [8192], P(('dp', 'fsdp'))
- query_grad: bfloat16 [8192, 4096], P('dp', 'fsdp')
The draws below stay inside these ranges and needn't reach their ends.
Inputs may be any that keep to these rules, and one draw needn't show every extreme that they name: `cand_blocks`: each query block lists 4 different passage blocks; block b is held by dp index b // 8. The blocks listed by the 4 query blocks of one dp index are all different, at most 1 of them are held by any one dp index, and some dp index holds exactly 1 of them. `positive`: position c names row c % 128 of the block in column c // 128 of the query's list.
All inputs are finite; a program needn't handle non-finite values.
Results may differ from the reference program's by a relative error of at most 0.0038.
Values may be sent and summed in bfloat16 or wider, within the bound.
No kernel may reach another device: no remote copies, remote signals or barrier semaphores. Data moves between devices by JAX's collectives and lax.ppermute only.
A program may use at most 64 MiB of HBM per device.

```python
from functools import partial
import jax
import jax.numpy as jnp
from jax import lax

D = 4096
BLK = 128
NLIST = 4
QB_DEV = 4
PB_DEV = 8
QBLOCKS = 64
PBLOCKS = 128
QUERIES = 8192
PASSAGES = 16384
N_DP = 16


def request_ids(key):
    base = jax.random.fold_in(key, 7)
    perm_keys = jax.random.split(jax.random.fold_in(base, 1), N_DP)
    orders = jax.vmap(partial(jax.random.permutation, x=N_DP))(perm_keys)
    request_count = NLIST * QB_DEV
    request_steps = jnp.arange(request_count)
    owners = orders[:, request_steps % N_DP]
    offsets = jax.random.randint(jax.random.fold_in(base, 2), (N_DP, N_DP), 0, PB_DEV)
    local_ids = (jnp.take_along_axis(offsets, owners, axis=1) + request_steps // N_DP) % PB_DEV
    return (owners * PB_DEV + local_ids).reshape(QBLOCKS, NLIST).astype(jnp.int32)


def passage_values(key):
    base = jax.random.fold_in(key, 13)
    values = jax.random.normal(jax.random.fold_in(base, 1), (PASSAGES, D), jnp.float32) * D ** (-0.5)
    return values


def query_values(key):
    base = jax.random.fold_in(key, 29)
    values = jax.random.normal(jax.random.fold_in(base, 1), (QUERIES, D), jnp.float32) * D ** (-0.5)
    return values


def draw_cand_blocks(key, part):
    return request_ids(key)


def draw_passage_emb(key, part):
    return passage_values(key).astype(jnp.bfloat16)


def draw_query_emb(key, part):
    return query_values(key).astype(jnp.bfloat16)


def place_ends(values, key, smallest, high):
    dims = values.shape
    spot = [jax.random.randint(jax.random.fold_in(key, axis), (), 0, dims[axis]) for axis in range(len(dims))]
    values = values.at[tuple(spot)].set(smallest)
    longest = dims.index(max(dims))
    spot[longest] = (spot[longest] + 1) % dims[longest]
    return values.at[tuple(spot)].set(high)


def setup_inputs(seed: int = 0) -> dict:
    streams_of = jax.random.split(jax.random.key(seed), 5)
    return {
        "query_emb": draw_query_emb(jax.random.fold_in(streams_of[4], 71), 0),
        "passage_emb": draw_passage_emb(jax.random.fold_in(streams_of[4], 71), 0),
        "cand_blocks": draw_cand_blocks(jax.random.fold_in(streams_of[4], 71), 0),
        "positive": place_ends(jax.random.randint(streams_of[3], (QUERIES,), 0, NLIST * BLK), jax.random.fold_in(streams_of[3], 1), 0, (NLIST * BLK) - 1).astype(jnp.int32),
    }


def softmax_rows(scores, positive_rows):
    row_max = jnp.max(scores, axis=1, keepdims=True)
    log_total = row_max[:, 0] + jnp.log(jnp.sum(jnp.exp(scores - row_max), axis=1))
    matched = lax.broadcasted_iota(jnp.int32, scores.shape, 1) == positive_rows[:, None]
    losses = log_total - jnp.sum(jnp.where(matched, scores, jnp.float32(0.0)), axis=1)
    weights = (jnp.exp(scores - log_total[:, None]) - matched.astype(jnp.float32)).astype(jnp.bfloat16)
    return losses, weights


def reference(query_emb, passage_emb, cand_blocks, positive):
    passage_blocks = passage_emb.reshape(PBLOCKS, BLK, D)
    query_blocks = query_emb.reshape(QBLOCKS, BLK, D)
    positive_blocks = positive.reshape(QBLOCKS, BLK)

    def one_block(inputs):
        query_rows, listed, positive_rows = inputs
        candidates = passage_blocks[listed].reshape(NLIST * BLK, D)
        scores = jnp.dot(query_rows, candidates.T, preferred_element_type=jnp.float32) * 50.0
        losses, weights = softmax_rows(scores, positive_rows)
        query_grad = (jnp.dot(weights, candidates, preferred_element_type=jnp.float32) * 50.0).astype(jnp.bfloat16)
        return losses, query_grad

    losses, query_grad = lax.map(one_block, (query_blocks, cand_blocks, positive_blocks))
    return losses.reshape(QUERIES), query_grad.reshape(QUERIES, D)
```

```python
import functools

import jax
import jax.numpy as jnp
from jax import lax
from jax.experimental import pallas as pl
from jax.experimental.pallas import tpu as pltpu
from jax.sharding import PartitionSpec as P

VMEM_LIMIT = 48 * 1024 * 1024
TILE = 512


def listed(slots_ref, block_ref, query_block, list_len):
    return jnp.concatenate(
        [block_ref[slots_ref[query_block, j]] for j in range(list_len)], axis=0
    )


def score_kernel(slots_ref, query_ref, block_ref, out_ref):
    query_blocks, list_len = slots_ref.shape
    block_rows = block_ref.shape[1]
    step = pl.program_id(0)
    for b in range(query_blocks):
        rows = pl.ds(b * block_rows, block_rows)
        share = lax.dot_general(
            query_ref[rows, :],
            listed(slots_ref, block_ref, b, list_len),
            (((1,), (1,)), ((), ())),
            preferred_element_type=jnp.float32,
        )

        @pl.when(step == 0)
        def _():
            out_ref[rows, :] = share

        @pl.when(step > 0)
        def _():
            out_ref[rows, :] += share


def partial_scores(slots, query_emb, blocks):
    query_blocks, list_len = slots.shape
    slot_count, block_rows, features = blocks.shape
    rows = query_emb.shape[0]
    tile = min(TILE, features)
    columns = list_len * block_rows
    return pl.pallas_call(
        score_kernel,
        out_shape=jax.ShapeDtypeStruct((rows, columns), jnp.float32),
        grid_spec=pltpu.PrefetchScalarGridSpec(
            num_scalar_prefetch=1,
            grid=(features // tile,),
            in_specs=[
                pl.BlockSpec((rows, tile), lambda t, s: (0, t)),
                pl.BlockSpec((slot_count, block_rows, tile), lambda t, s: (0, 0, t)),
            ],
            out_specs=pl.BlockSpec((rows, columns), lambda t, s: (0, 0)),
        ),
        compiler_params=pltpu.CompilerParams(vmem_limit_bytes=VMEM_LIMIT),
        cost_estimate=pl.CostEstimate(
            flops=2 * rows * columns * features,
            bytes_accessed=2 * blocks.size + 2 * query_emb.size + 4 * rows * columns,
            transcendentals=0,
        ),
        name="partial_scores",
    )(slots, query_emb, blocks)


def gradient_kernel(
    share_count, slots_ref, first_ref, positive_ref, *refs
):
    share_refs = refs[:share_count]
    block_ref, loss_ref, grad_ref, weight_ref, all_loss_ref = refs[share_count:]
    query_blocks, list_len = slots_ref.shape
    block_rows = block_ref.shape[1]

    @pl.when(pl.program_id(0) == 0)
    def _():
        for b in range(query_blocks):
            rows = pl.ds(b * block_rows, block_rows)
            total = share_refs[0][rows, :]
            for ref in share_refs[1:]:
                total = total + ref[rows, :]
            scores = total * 50.0
            row_max = jnp.max(scores, axis=1, keepdims=True)
            log_total = row_max + jnp.log(
                jnp.sum(jnp.exp(scores - row_max), axis=1, keepdims=True)
            )
            matched = (
                lax.broadcasted_iota(jnp.int32, scores.shape, 1) == positive_ref[rows, :]
            )
            picked = jnp.sum(jnp.where(matched, scores, 0.0), axis=1, keepdims=True)
            all_loss_ref[rows, :] = log_total - picked
            weight_ref[rows, :] = (
                jnp.exp(scores - log_total) - matched.astype(jnp.float32)
            ).astype(jnp.bfloat16)
        loss_ref[...] = all_loss_ref[pl.ds(first_ref[0], loss_ref.shape[0]), :]

    for b in range(query_blocks):
        rows = pl.ds(b * block_rows, block_rows)
        grad = jnp.dot(
            weight_ref[rows, :],
            listed(slots_ref, block_ref, b, list_len),
            preferred_element_type=jnp.float32,
        )
        grad_ref[rows, :] = (grad * 50.0).astype(jnp.bfloat16)


def losses_and_gradients(slots, first_row, share_rows, positive, shares, blocks):
    slot_count, block_rows, features = blocks.shape
    rows, columns = shares[0].shape
    tile = min(TILE, features)
    whole = lambda t, s, f: (0, 0)
    return pl.pallas_call(
        functools.partial(gradient_kernel, len(shares)),
        out_shape=(
            jax.ShapeDtypeStruct((share_rows, 1), jnp.float32),
            jax.ShapeDtypeStruct((rows, features), jnp.bfloat16),
        ),
        grid_spec=pltpu.PrefetchScalarGridSpec(
            num_scalar_prefetch=2,
            grid=(features // tile,),
            in_specs=[pl.BlockSpec((rows, 1), whole)]
            + [pl.BlockSpec((rows, columns), whole)] * len(shares)
            + [pl.BlockSpec((slot_count, block_rows, tile), lambda t, s, f: (0, 0, t))],
            out_specs=[
                pl.BlockSpec((share_rows, 1), whole),
                pl.BlockSpec((rows, tile), lambda t, s, f: (0, t)),
            ],
            scratch_shapes=[
                pltpu.VMEM((rows, columns), jnp.bfloat16),
                pltpu.VMEM((rows, 1), jnp.float32),
            ],
        ),
        compiler_params=pltpu.CompilerParams(vmem_limit_bytes=VMEM_LIMIT),
        cost_estimate=pl.CostEstimate(
            flops=2 * rows * columns * features,
            bytes_accessed=2 * blocks.size + 2 * rows * features + 8 * rows * columns,
            transcendentals=2 * rows * columns,
        ),
        name="losses_and_gradients",
    )(slots, first_row, positive.reshape(rows, 1), *shares, blocks)


def shards(query_emb, passage_emb, cand_blocks, positive):
    dp_count = lax.axis_size("dp")
    fsdp_count = lax.axis_size("fsdp")
    query_blocks, list_len = cand_blocks.shape
    row_count, feature_count = query_emb.shape
    block_rows = row_count // query_blocks
    passage_blocks = passage_emb.shape[0] // block_rows
    owners = cand_blocks // passage_blocks
    local_ids = cand_blocks % passage_blocks
    owner_index = lax.broadcasted_iota(jnp.int32, (dp_count, query_blocks, list_len), 0)
    id_table = jnp.sum(jnp.where(owner_index == owners[None], local_ids[None], 0), axis=(1, 2))
    requested = lax.all_to_all(
        id_table.reshape(dp_count, 1), "dp", split_axis=0, concat_axis=0, tiled=True
    ).reshape(dp_count)
    stored = passage_emb.reshape(passage_blocks, block_rows, feature_count)
    fetched = lax.all_to_all(stored[requested], "dp", split_axis=0, concat_axis=0, tiled=True)
    mine = partial_scores(owners, query_emb, fetched)
    shares = [mine] + [
        lax.ppermute(mine, "fsdp", [(i, (i + k) % fsdp_count) for i in range(fsdp_count)])
        for k in range(1, fsdp_count)
    ]
    share_rows = row_count // fsdp_count
    first_row = (lax.axis_index("fsdp") * share_rows).astype(jnp.int32).reshape(1)
    losses, query_grad = losses_and_gradients(
        owners, first_row, share_rows, positive, shares, fetched
    )
    return losses.reshape(share_rows), query_grad


def solution(mesh):
    return jax.shard_map(
        shards,
        mesh=mesh,
        in_specs=(P("dp", "fsdp"), P("dp", "fsdp"), P("dp", None), P("dp")),
        out_specs=(P(("dp", "fsdp")), P("dp", "fsdp")),
        check_vma=False,
    )
```

```python
import functools

import jax
import jax.numpy as jnp
from jax import lax
from jax.experimental import pallas as pl
from jax.experimental.pallas import tpu as pltpu
from jax.sharding import PartitionSpec as P

VMEM_LIMIT = 32 * 1024 * 1024
TILE = 512
LANES = 128
WINDOW = 8
SHIFT = 1 << 16
IN_VMEM = pl.BlockSpec(memory_space=pltpu.VMEM)
IN_HBM = pl.BlockSpec(memory_space=pltpu.HBM)
IN_SMEM = pl.BlockSpec(memory_space=pltpu.SMEM)


def hbm(array):
    return pltpu.with_memory_space_constraint(array, pltpu.HBM)


def vmem(array):
    return pltpu.with_memory_space_constraint(array, pltpu.VMEM)


def run_copies(copies):
    for copy in copies:
        copy.start()
    for copy in copies:
        copy.wait()


def pick_kernel(ids_ref, stored_ref, out_ref, held_ref, loaded, done):
    count, block_rows, features = out_ref.shape
    first = stored_ref.shape[1] - features
    loads = [
        pltpu.make_async_copy(
            stored_ref.at[
                pl.ds(pl.multiple_of(ids_ref[i] * block_rows, block_rows), block_rows),
                pl.ds(first, features),
            ],
            held_ref.at[i],
            loaded.at[i],
        )
        for i in range(count)
    ]
    stores = [
        pltpu.make_async_copy(held_ref.at[i], out_ref.at[i], done.at[i]) for i in range(count)
    ]
    for load in loads[:WINDOW]:
        load.start()
    for i in range(count):
        loads[i].wait()
        stores[i].start()
        if i + WINDOW < count:
            loads[i + WINDOW].start()
    for store in stores:
        store.wait()


def pick_blocks(ids, passage_emb, block_rows, first):
    count, features = ids.shape[0], passage_emb.shape[1] - first
    return pl.pallas_call(
        pick_kernel,
        out_shape=pltpu.HBM((count, block_rows, features), passage_emb.dtype),
        in_specs=[IN_SMEM, IN_HBM],
        out_specs=IN_HBM,
        scratch_shapes=[
            pltpu.VMEM((count, block_rows, features), passage_emb.dtype),
            pltpu.SemaphoreType.DMA((count,)),
            pltpu.SemaphoreType.DMA((count,)),
        ],
        compiler_params=pltpu.CompilerParams(vmem_limit_bytes=VMEM_LIMIT),
        cost_estimate=pl.CostEstimate(
            flops=0, bytes_accessed=4 * count * block_rows * features, transcendentals=0
        ),
        name="pick_blocks",
    )(ids, hbm(passage_emb))


def pick_pairs_kernel(ids_ref, stored_ref, *refs):
    *far_refs, out_ref, done = refs
    count, _, block_rows, features = out_ref.shape
    copies = []

    def add(source, item, which, first, width):
        rows = pl.ds(pl.multiple_of(ids_ref[item, which] * block_rows, block_rows), block_rows)
        copies.append(
            pltpu.make_async_copy(
                source.at[rows, pl.ds(0, width)],
                out_ref.at[item, which, :, pl.ds(first, width)],
                done.at[len(copies)],
            )
        )

    for item in range(count):
        add(stored_ref, item, 0, 0, features)
        first = 0
        for far_ref in far_refs:
            add(far_ref, item, 1, first, far_ref.shape[1])
            first += far_ref.shape[1]
    run_copies(copies)


def pick_pairs(ids, passage_emb, far_parts, block_rows):
    count = ids.shape[0]
    features = sum(part.shape[1] for part in far_parts)
    return pl.pallas_call(
        pick_pairs_kernel,
        out_shape=pltpu.VMEM((count, 2, block_rows, features), passage_emb.dtype),
        in_specs=[IN_SMEM] + [IN_HBM] * (1 + len(far_parts)),
        out_specs=IN_VMEM,
        scratch_shapes=[pltpu.SemaphoreType.DMA((count * (1 + len(far_parts)),))],
        compiler_params=pltpu.CompilerParams(vmem_limit_bytes=VMEM_LIMIT),
        cost_estimate=pl.CostEstimate(flops=10**12, bytes_accessed=10**9, transcendentals=0),
        name="pick_pairs",
    )(ids, hbm(passage_emb), *[hbm(part) for part in far_parts])


def score_kernel(
    near_slots_ref, slots_ref, query_ref, positive_ref, near_ref, fetched_ref, *refs
):
    score_ref, listed_ref, held_positive_ref, near_done, done = refs
    query_blocks, list_len = slots_ref.shape
    block_rows, near_features = near_ref.shape[1:]
    held_positive_ref[...] = positive_ref[...]
    copies = []
    for b in range(query_blocks):
        for j in range(list_len):
            i = b * list_len + j
            for source_ref, table_ref, first, arrived in (
                (near_ref, near_slots_ref, 0, near_done),
                (fetched_ref, slots_ref, near_features, done),
            ):
                copies.append(
                    pltpu.make_async_copy(
                        source_ref.at[table_ref[b, j]],
                        listed_ref.at[i, :, pl.ds(first, source_ref.shape[2])],
                        arrived.at[i],
                    )
                )
    for copy in copies:
        copy.start()
    for b in range(query_blocks):
        for copy in copies[2 * b * list_len : 2 * (b + 1) * list_len]:
            copy.wait()
        listed = listed_ref[b * list_len : (b + 1) * list_len]
        score_ref[b] = lax.dot_general(
            query_ref[b * block_rows : (b + 1) * block_rows, :],
            listed.reshape(list_len * block_rows, listed.shape[2]),
            (((1,), (1,)), ((), ())),
            preferred_element_type=jnp.float32,
        )


def partial_scores(near_slots, slots, query_emb, positive, near, fetched):
    query_blocks, list_len = slots.shape
    block_rows = fetched.shape[1]
    features = query_emb.shape[1]
    columns = list_len * block_rows
    listed_count = query_blocks * list_len
    return pl.pallas_call(
        score_kernel,
        out_shape=(
            pltpu.VMEM((query_blocks, block_rows, columns), jnp.float32),
            pltpu.VMEM((listed_count, block_rows, features), fetched.dtype),
            pltpu.VMEM((query_blocks, 1, block_rows), jnp.int32),
        ),
        in_specs=[IN_SMEM] * 2 + [IN_VMEM] * 2 + [IN_HBM] * 2,
        out_specs=[IN_VMEM] * 3,
        scratch_shapes=[pltpu.SemaphoreType.DMA((listed_count,))] * 2,
        compiler_params=pltpu.CompilerParams(vmem_limit_bytes=VMEM_LIMIT),
        cost_estimate=pl.CostEstimate(
            flops=2 * query_blocks * block_rows * columns * features,
            bytes_accessed=2 * listed_count * block_rows * features + 2 * query_emb.size,
            transcendentals=0,
        ),
        name="partial_scores",
    )(
        near_slots,
        slots,
        query_emb,
        positive.reshape(query_blocks, 1, block_rows),
        hbm(near),
        hbm(fetched),
    )


def gradient_kernel(share_count, share_ref, *refs):
    score_refs = refs[:share_count]
    listed_ref, positive_ref, loss_ref, grad_ref = refs[share_count:]
    block = pl.program_id(0)
    block_rows, features = grad_ref.shape
    list_len = listed_ref.shape[0] // pl.num_programs(0)
    total = score_refs[0][block]
    for ref in score_refs[1:]:
        total = total + ref[block]
    scores = total * 50.0
    row_max = jnp.max(scores, axis=1, keepdims=True)
    log_total = row_max + jnp.log(jnp.sum(jnp.exp(scores - row_max), axis=1, keepdims=True))
    square = (block_rows, block_rows)
    positive = jnp.broadcast_to(positive_ref[block], square).T[:, :1]
    matched = lax.broadcasted_iota(jnp.int32, scores.shape, 1) == positive
    picked = jnp.sum(jnp.where(matched, scores, 0.0), axis=1, keepdims=True)
    losses = jnp.broadcast_to(log_total - picked, square).T[:1]
    held = loss_ref.shape[0]

    @pl.when(block // held == share_ref[0])
    def _():
        loss_ref[block % held] = losses

    weights = (jnp.exp(scores - log_total) - matched.astype(jnp.float32)).astype(jnp.bfloat16)
    tile = min(TILE, features)
    for f in range(0, features, tile):
        listed = listed_ref[pl.ds(block * list_len, list_len), :, f : f + tile]
        grad = jnp.dot(
            weights,
            listed.reshape(list_len * block_rows, tile),
            preferred_element_type=jnp.float32,
        )
        grad_ref[:, f : f + tile] = (grad * 50.0).astype(jnp.bfloat16)


def losses_and_gradients(share, share_blocks, scores, listed, positive):
    query_blocks, block_rows, columns = scores[0].shape
    features = listed.shape[2]
    rows = query_blocks * block_rows
    return pl.pallas_call(
        functools.partial(gradient_kernel, len(scores)),
        out_shape=(
            jax.ShapeDtypeStruct((share_blocks, 1, block_rows), jnp.float32),
            jax.ShapeDtypeStruct((rows, features), jnp.bfloat16),
        ),
        grid=(query_blocks,),
        in_specs=[IN_SMEM] + [IN_VMEM] * (len(scores) + 2),
        out_specs=[
            pl.BlockSpec((share_blocks, 1, block_rows), lambda b: (0, 0, 0)),
            pl.BlockSpec((block_rows, features), lambda b: (b, 0)),
        ],
        compiler_params=pltpu.CompilerParams(vmem_limit_bytes=VMEM_LIMIT),
        cost_estimate=pl.CostEstimate(
            flops=2 * rows * columns * features,
            bytes_accessed=2 * rows * features,
            transcendentals=2 * rows * columns,
        ),
        name="losses_and_gradients",
    )(share, *[vmem(score) for score in scores], vmem(listed), vmem(positive))


def shards(query_emb, passage_emb, cand_blocks, positive):
    dp_count = lax.axis_size("dp")
    fsdp_count = lax.axis_size("fsdp")
    query_blocks, list_len = cand_blocks.shape
    row_count, feature_count = query_emb.shape
    block_rows = row_count // query_blocks
    passage_blocks = passage_emb.shape[0] // block_rows
    half = dp_count // 2
    me = lax.axis_index("dp")
    me_in_half = me % half
    owners = cand_blocks // passage_blocks
    local_ids = cand_blocks % passage_blocks

    share = lax.axis_index("fsdp").astype(jnp.int32)
    to_other_half = [(d, (d + half) % dp_count) for d in range(dp_count)]
    first = LANES
    swapped = first + max(1, feature_count // LANES * 3 // 16) * LANES
    early_half = lax.ppermute(passage_emb[:, :first], "dp", to_other_half)

    owner_index = lax.broadcasted_iota(jnp.int32, (dp_count, query_blocks, list_len), 0)
    other_half = (owner_index + half) % dp_count == owners[None]
    both_ids = jnp.where(owner_index == owners[None], local_ids[None], 0) + jnp.where(
        other_half, SHIFT * local_ids[None], 0
    )
    both_tables = jnp.sum(both_ids, axis=(1, 2)).reshape(dp_count, 1)
    both_tables, share = lax.optimization_barrier((both_tables, share))
    requested = lax.all_to_all(both_tables, "dp", split_axis=0, concat_axis=0, tiled=True)
    requested = requested.reshape(dp_count)
    requested, early_half = lax.optimization_barrier((requested, early_half))
    late_half, requested = lax.optimization_barrier((passage_emb[:, first:swapped], requested))
    far_parts = [early_half, lax.ppermute(late_half, "dp", to_other_half)]
    picked = pick_blocks(requested % SHIFT, passage_emb, block_rows, swapped)
    fetched = lax.all_to_all(picked, "dp", split_axis=0, concat_axis=0, tiled=True)

    steps = jnp.arange(half, dtype=jnp.int32)
    readers = me - me_in_half + (me_in_half + steps) % half
    relayed = requested[readers]
    relayed = jnp.stack([relayed % SHIFT, relayed // SHIFT], axis=1)
    pairs = pick_pairs(relayed, passage_emb, far_parts, block_rows)
    near = jnp.concatenate(
        [pairs[0]]
        + [
            lax.ppermute(
                pairs[k],
                "dp",
                [(d, d - d % half + (d % half + k) % half) for d in range(dp_count)],
            )
            for k in range(1, half)
        ],
        axis=0,
    )
    near_slots = 2 * ((me_in_half - owners) % half) + (owners // half != me // half)
    near_slots = near_slots.astype(jnp.int32)

    mine, listed, positive = partial_scores(
        near_slots, owners, query_emb, positive, near, fetched
    )
    scores = [mine] + [
        lax.ppermute(mine, "fsdp", [(i, (i + k) % fsdp_count) for i in range(fsdp_count)])
        for k in range(1, fsdp_count)
    ]
    share_rows = row_count // fsdp_count
    if share_rows % block_rows == 0:
        losses, query_grad = losses_and_gradients(
            share.reshape(1), share_rows // block_rows, scores, listed, positive
        )
        return losses.reshape(share_rows), query_grad
    whole = jnp.zeros((1,), jnp.int32)
    losses, query_grad = losses_and_gradients(whole, query_blocks, scores, listed, positive)
    losses = lax.dynamic_slice_in_dim(losses.reshape(row_count), share * share_rows, share_rows)
    return losses, query_grad


def solution(mesh):
    return jax.shard_map(
        shards,
        mesh=mesh,
        in_specs=(P("dp", "fsdp"), P("dp", "fsdp"), P("dp", None), P("dp")),
        out_specs=(P(("dp", "fsdp")), P("dp", "fsdp")),
        check_vma=False,
    )
```

```python
import functools

import jax
import jax.numpy as jnp
from jax import lax
from jax.experimental import pallas as pl
from jax.experimental.pallas import tpu as pltpu
from jax.sharding import PartitionSpec as P

VMEM_LIMIT = 32 * 1024 * 1024
TILE = 512
LANES = 128
WINDOW = 8
SHIFT = 1 << 16
IN_VMEM = pl.BlockSpec(memory_space=pltpu.VMEM)
IN_HBM = pl.BlockSpec(memory_space=pltpu.HBM)
IN_SMEM = pl.BlockSpec(memory_space=pltpu.SMEM)


def hbm(array):
    return pltpu.with_memory_space_constraint(array, pltpu.HBM)


def vmem(array):
    return pltpu.with_memory_space_constraint(array, pltpu.VMEM)


def run_copies(copies):
    for copy in copies:
        copy.start()
    for copy in copies:
        copy.wait()


def pick_kernel(ids_ref, stored_ref, out_ref, held_ref, loaded, done):
    count, block_rows, features = out_ref.shape
    first = stored_ref.shape[1] - features
    loads = [
        pltpu.make_async_copy(
            stored_ref.at[
                pl.ds(pl.multiple_of(ids_ref[i] * block_rows, block_rows), block_rows),
                pl.ds(first, features),
            ],
            held_ref.at[i],
            loaded.at[i],
        )
        for i in range(count)
    ]
    stores = [
        pltpu.make_async_copy(held_ref.at[i], out_ref.at[i], done.at[i]) for i in range(count)
    ]
    for load in loads[:WINDOW]:
        load.start()
    for i in range(count):
        loads[i].wait()
        stores[i].start()
        if i + WINDOW < count:
            loads[i + WINDOW].start()
    for store in stores:
        store.wait()


def pick_blocks(ids, passage_emb, block_rows, first):
    count, features = ids.shape[0], passage_emb.shape[1] - first
    return pl.pallas_call(
        pick_kernel,
        out_shape=pltpu.HBM((count, block_rows, features), passage_emb.dtype),
        in_specs=[IN_SMEM, IN_HBM],
        out_specs=IN_HBM,
        scratch_shapes=[
            pltpu.VMEM((count, block_rows, features), passage_emb.dtype),
            pltpu.SemaphoreType.DMA((count,)),
            pltpu.SemaphoreType.DMA((count,)),
        ],
        compiler_params=pltpu.CompilerParams(vmem_limit_bytes=VMEM_LIMIT),
        cost_estimate=pl.CostEstimate(
            flops=0, bytes_accessed=4 * count * block_rows * features, transcendentals=0
        ),
        name="pick_blocks",
    )(ids, hbm(passage_emb))


def pick_pairs_kernel(ids_ref, stored_ref, *refs):
    *far_refs, out_ref, done = refs
    count, _, block_rows, features = out_ref.shape
    copies = []

    def add(source, item, which, first, width):
        rows = pl.ds(pl.multiple_of(ids_ref[item, which] * block_rows, block_rows), block_rows)
        copies.append(
            pltpu.make_async_copy(
                source.at[rows, pl.ds(0, width)],
                out_ref.at[item, which, :, pl.ds(first, width)],
                done.at[len(copies)],
            )
        )

    for item in range(count):
        add(stored_ref, item, 0, 0, features)
        first = 0
        for far_ref in far_refs:
            add(far_ref, item, 1, first, far_ref.shape[1])
            first += far_ref.shape[1]
    run_copies(copies)


def pick_pairs(ids, passage_emb, far_parts, block_rows):
    count = ids.shape[0]
    features = sum(part.shape[1] for part in far_parts)
    return pl.pallas_call(
        pick_pairs_kernel,
        out_shape=pltpu.VMEM((count, 2, block_rows, features), passage_emb.dtype),
        in_specs=[IN_SMEM] + [IN_HBM] * (1 + len(far_parts)),
        out_specs=IN_VMEM,
        scratch_shapes=[pltpu.SemaphoreType.DMA((count * (1 + len(far_parts)),))],
        compiler_params=pltpu.CompilerParams(vmem_limit_bytes=VMEM_LIMIT),
        cost_estimate=pl.CostEstimate(flops=10**12, bytes_accessed=10**9, transcendentals=0),
        name="pick_pairs",
    )(ids, hbm(passage_emb), *[hbm(part) for part in far_parts])


def block_copies(table_ref, block, source_ref, listed_ref, first, done):
    list_len = table_ref.shape[1]
    features = source_ref.shape[2]
    return [
        pltpu.make_async_copy(
            source_ref.at[table_ref[block, j]],
            listed_ref.at[block * list_len + j, :, pl.ds(first, features)],
            done.at[block * list_len + j],
        )
        for j in range(list_len)
    ]


def block_scores(query_ref, listed_ref, block, list_len, first, features):
    block_rows = listed_ref.shape[1]
    listed = listed_ref[block * list_len : (block + 1) * list_len, :, first : first + features]
    return lax.dot_general(
        query_ref[block * block_rows : (block + 1) * block_rows, first : first + features],
        listed.reshape(list_len * block_rows, features),
        (((1,), (1,)), ((), ())),
        preferred_element_type=jnp.float32,
    )


def near_score_kernel(near_slots_ref, query_ref, near_ref, score_ref, listed_ref, done):
    query_blocks, list_len = near_slots_ref.shape
    copies = [
        block_copies(near_slots_ref, b, near_ref, listed_ref, 0, done)
        for b in range(query_blocks)
    ]
    for copy in sum(copies, []):
        copy.start()
    for b in range(query_blocks):
        for copy in copies[b]:
            copy.wait()
        score_ref[b] = block_scores(query_ref, listed_ref, b, list_len, 0, near_ref.shape[2])


def near_scores(near_slots, query_emb, near):
    query_blocks, list_len = near_slots.shape
    _, block_rows, features = near.shape
    columns = list_len * block_rows
    listed_count = query_blocks * list_len
    return pl.pallas_call(
        near_score_kernel,
        out_shape=jax.ShapeDtypeStruct((query_blocks, block_rows, columns), jnp.float32),
        in_specs=[IN_SMEM, IN_VMEM, IN_HBM],
        out_specs=IN_VMEM,
        scratch_shapes=[
            pltpu.VMEM((listed_count, block_rows, features), near.dtype),
            pltpu.SemaphoreType.DMA((listed_count,)),
        ],
        compiler_params=pltpu.CompilerParams(vmem_limit_bytes=VMEM_LIMIT),
        cost_estimate=pl.CostEstimate(
            flops=2 * query_blocks * block_rows * columns * features,
            bytes_accessed=2 * listed_count * block_rows * features + 2 * query_emb.size,
            transcendentals=0,
        ),
        name="near_scores",
    )(near_slots, query_emb, hbm(near))


def score_kernel(
    near_slots_ref, slots_ref, query_ref, positive_ref, before_ref, near_ref, fetched_ref, *refs
):
    score_ref, listed_ref, held_positive_ref, near_done, done = refs
    query_blocks, list_len = slots_ref.shape
    near_features, features = near_ref.shape[2], fetched_ref.shape[2]
    blocks = range(query_blocks)
    copies = [
        block_copies(slots_ref, b, fetched_ref, listed_ref, near_features, done) for b in blocks
    ]
    near_copies = [
        block_copies(near_slots_ref, b, near_ref, listed_ref, 0, near_done) for b in blocks
    ]
    for copy in sum(copies + near_copies, []):
        copy.start()
    held_positive_ref[...] = positive_ref[...]
    for b in blocks:
        for copy in copies[b]:
            copy.wait()
        score_ref[b] = before_ref[b] + block_scores(
            query_ref, listed_ref, b, list_len, near_features, features
        )
    for copy in sum(near_copies, []):
        copy.wait()


def partial_scores(near_slots, slots, query_emb, positive, before, near, fetched):
    query_blocks, list_len = slots.shape
    block_rows = fetched.shape[1]
    features = query_emb.shape[1]
    columns = list_len * block_rows
    listed_count = query_blocks * list_len
    return pl.pallas_call(
        score_kernel,
        out_shape=(
            pltpu.VMEM((query_blocks, block_rows, columns), jnp.float32),
            pltpu.VMEM((listed_count, block_rows, features), fetched.dtype),
            pltpu.VMEM((query_blocks, 1, block_rows), jnp.int32),
        ),
        in_specs=[IN_SMEM] * 2 + [IN_VMEM] * 3 + [IN_HBM] * 2,
        out_specs=[IN_VMEM] * 3,
        scratch_shapes=[pltpu.SemaphoreType.DMA((listed_count,))] * 2,
        compiler_params=pltpu.CompilerParams(vmem_limit_bytes=VMEM_LIMIT),
        cost_estimate=pl.CostEstimate(
            flops=2 * query_blocks * block_rows * columns * fetched.shape[2],
            bytes_accessed=2 * listed_count * block_rows * features + 2 * query_emb.size,
            transcendentals=0,
        ),
        name="partial_scores",
    )(
        near_slots,
        slots,
        query_emb,
        positive.reshape(query_blocks, 1, block_rows),
        before,
        hbm(near),
        hbm(fetched),
    )


def gradient_kernel(share_count, share_ref, *refs):
    score_refs = refs[:share_count]
    listed_ref, positive_ref, loss_ref, grad_ref = refs[share_count:]
    block = pl.program_id(0)
    block_rows, features = grad_ref.shape
    list_len = listed_ref.shape[0] // pl.num_programs(0)
    total = score_refs[0][block]
    for ref in score_refs[1:]:
        total = total + ref[block]
    scores = total * 50.0
    row_max = jnp.max(scores, axis=1, keepdims=True)
    log_total = row_max + jnp.log(jnp.sum(jnp.exp(scores - row_max), axis=1, keepdims=True))
    square = (block_rows, block_rows)
    positive = jnp.broadcast_to(positive_ref[block], square).T[:, :1]
    matched = lax.broadcasted_iota(jnp.int32, scores.shape, 1) == positive
    picked = jnp.sum(jnp.where(matched, scores, 0.0), axis=1, keepdims=True)
    losses = jnp.broadcast_to(log_total - picked, square).T[:1]
    held = loss_ref.shape[0]

    @pl.when(block // held == share_ref[0])
    def _():
        loss_ref[block % held] = losses

    weights = (jnp.exp(scores - log_total) - matched.astype(jnp.float32)).astype(jnp.bfloat16)
    tile = min(TILE, features)
    for f in range(0, features, tile):
        listed = listed_ref[pl.ds(block * list_len, list_len), :, f : f + tile]
        grad = jnp.dot(
            weights,
            listed.reshape(list_len * block_rows, tile),
            preferred_element_type=jnp.float32,
        )
        grad_ref[:, f : f + tile] = (grad * 50.0).astype(jnp.bfloat16)


def losses_and_gradients(share, share_blocks, scores, listed, positive):
    query_blocks, block_rows, columns = scores[0].shape
    features = listed.shape[2]
    rows = query_blocks * block_rows
    return pl.pallas_call(
        functools.partial(gradient_kernel, len(scores)),
        out_shape=(
            jax.ShapeDtypeStruct((share_blocks, 1, block_rows), jnp.float32),
            jax.ShapeDtypeStruct((rows, features), jnp.bfloat16),
        ),
        grid=(query_blocks,),
        in_specs=[IN_SMEM] + [IN_VMEM] * (len(scores) + 2),
        out_specs=[
            pl.BlockSpec((share_blocks, 1, block_rows), lambda b: (0, 0, 0)),
            pl.BlockSpec((block_rows, features), lambda b: (b, 0)),
        ],
        compiler_params=pltpu.CompilerParams(vmem_limit_bytes=VMEM_LIMIT),
        cost_estimate=pl.CostEstimate(
            flops=2 * rows * columns * features,
            bytes_accessed=2 * rows * features,
            transcendentals=2 * rows * columns,
        ),
        name="losses_and_gradients",
    )(share, *[vmem(score) for score in scores], vmem(listed), vmem(positive))


def shards(query_emb, passage_emb, cand_blocks, positive):
    dp_count = lax.axis_size("dp")
    fsdp_count = lax.axis_size("fsdp")
    query_blocks, list_len = cand_blocks.shape
    row_count, feature_count = query_emb.shape
    block_rows = row_count // query_blocks
    passage_blocks = passage_emb.shape[0] // block_rows
    half = dp_count // 2
    me = lax.axis_index("dp")
    me_in_half = me % half
    owners = cand_blocks // passage_blocks
    local_ids = cand_blocks % passage_blocks

    share = lax.axis_index("fsdp").astype(jnp.int32)
    far = half + half // 2
    to_other_half = [(d, d ^ far) for d in range(dp_count)]
    first = LANES
    swapped = first + max(1, feature_count // LANES * 3 // 16) * LANES
    early_half = lax.ppermute(passage_emb[:, :first], "dp", to_other_half)

    owner_index = lax.broadcasted_iota(jnp.int32, (dp_count, query_blocks, list_len), 0)
    other_half = (owner_index ^ far) == owners[None]
    both_ids = jnp.where(owner_index == owners[None], local_ids[None], 0) + jnp.where(
        other_half, SHIFT * local_ids[None], 0
    )
    both_tables = jnp.sum(both_ids, axis=(1, 2)).reshape(dp_count, 1)
    both_tables, share = lax.optimization_barrier((both_tables, share))
    requested = lax.all_to_all(both_tables, "dp", split_axis=0, concat_axis=0, tiled=True)
    requested = requested.reshape(dp_count)
    requested, early_half = lax.optimization_barrier((requested, early_half))
    late_half, requested = lax.optimization_barrier((passage_emb[:, first:swapped], requested))
    far_parts = [early_half, lax.ppermute(late_half, "dp", to_other_half)]
    quarter = dp_count // 4
    order = [quarter * z + c for c in range(quarter) for z in (0, 3, 1, 2)]
    slots = jnp.asarray([order.index(d) for d in range(dp_count)], jnp.int32)[owners]
    picked = pick_blocks(
        (requested % SHIFT)[jnp.asarray(order, jnp.int32)], passage_emb, block_rows, swapped
    )
    fetched = lax.all_to_all(
        picked, "dp", split_axis=0, concat_axis=0, tiled=True, axis_index_groups=[order]
    )

    steps = jnp.arange(half, dtype=jnp.int32)
    readers = me - me_in_half + (me_in_half + steps) % half
    relayed = requested[readers]
    relayed = jnp.stack([relayed % SHIFT, relayed // SHIFT], axis=1)
    pairs = pick_pairs(relayed, passage_emb, far_parts, block_rows)
    near = jnp.concatenate(
        [pairs[0]]
        + [
            lax.ppermute(
                pairs[k],
                "dp",
                [(d, d - d % half + (d % half + k) % half) for d in range(dp_count)],
            )
            for k in range(1, half)
        ],
        axis=0,
    )
    is_far = (owners // half != me // half).astype(jnp.int32)
    near_slots = 2 * ((me - (owners ^ (far * is_far))) % half) + is_far
    near_slots = near_slots.astype(jnp.int32)

    before = near_scores(near_slots, query_emb, near)
    mine, listed, positive = partial_scores(
        near_slots, slots, query_emb, positive, before, near, fetched
    )
    scores = [mine] + [
        lax.ppermute(mine, "fsdp", [(i, (i + k) % fsdp_count) for i in range(fsdp_count)])
        for k in range(1, fsdp_count)
    ]
    share_rows = row_count // fsdp_count
    if share_rows % block_rows == 0:
        losses, query_grad = losses_and_gradients(
            share.reshape(1), share_rows // block_rows, scores, listed, positive
        )
        return losses.reshape(share_rows), query_grad
    whole = jnp.zeros((1,), jnp.int32)
    losses, query_grad = losses_and_gradients(whole, query_blocks, scores, listed, positive)
    losses = lax.dynamic_slice_in_dim(losses.reshape(row_count), share * share_rows, share_rows)
    return losses, query_grad


def solution(mesh):
    return jax.shard_map(
        shards,
        mesh=mesh,
        in_specs=(P("dp", "fsdp"), P("dp", "fsdp"), P("dp", None), P("dp")),
        out_specs=(P(("dp", "fsdp")), P("dp", "fsdp")),
        check_vma=False,
    )
```

```python
import functools

import jax
import jax.numpy as jnp
from jax import lax
from jax.experimental import pallas as pl
from jax.experimental.pallas import tpu as pltpu
from jax.sharding import PartitionSpec as P

VMEM_LIMIT = 32 * 1024 * 1024
TILE = 512
LANES = 128
WINDOW = 8
SHIFT = 1 << 16
IN_VMEM = pl.BlockSpec(memory_space=pltpu.VMEM)
IN_HBM = pl.BlockSpec(memory_space=pltpu.HBM)
IN_SMEM = pl.BlockSpec(memory_space=pltpu.SMEM)


def hbm(array):
    return pltpu.with_memory_space_constraint(array, pltpu.HBM)


def vmem(array):
    return pltpu.with_memory_space_constraint(array, pltpu.VMEM)


def run_copies(copies):
    for copy in copies:
        copy.start()
    for copy in copies:
        copy.wait()


def pick_kernel(ids_ref, stored_ref, out_ref, held_ref, loaded, done):
    count, block_rows, features = out_ref.shape
    first = stored_ref.shape[1] - features
    loads = [
        pltpu.make_async_copy(
            stored_ref.at[
                pl.ds(pl.multiple_of(ids_ref[i] * block_rows, block_rows), block_rows),
                pl.ds(first, features),
            ],
            held_ref.at[i],
            loaded.at[i],
        )
        for i in range(count)
    ]
    stores = [
        pltpu.make_async_copy(held_ref.at[i], out_ref.at[i], done.at[i]) for i in range(count)
    ]
    for load in loads[:WINDOW]:
        load.start()
    for i in range(count):
        loads[i].wait()
        stores[i].start()
        if i + WINDOW < count:
            loads[i + WINDOW].start()
    for store in stores:
        store.wait()


def pick_blocks(ids, passage_emb, block_rows, first):
    count, features = ids.shape[0], passage_emb.shape[1] - first
    return pl.pallas_call(
        pick_kernel,
        out_shape=pltpu.HBM((count, block_rows, features), passage_emb.dtype),
        in_specs=[IN_SMEM, IN_HBM],
        out_specs=IN_HBM,
        scratch_shapes=[
            pltpu.VMEM((count, block_rows, features), passage_emb.dtype),
            pltpu.SemaphoreType.DMA((count,)),
            pltpu.SemaphoreType.DMA((count,)),
        ],
        compiler_params=pltpu.CompilerParams(vmem_limit_bytes=VMEM_LIMIT),
        cost_estimate=pl.CostEstimate(
            flops=0, bytes_accessed=4 * count * block_rows * features, transcendentals=0
        ),
        name="pick_blocks",
    )(ids, hbm(passage_emb))


def pick_pairs_kernel(ids_ref, stored_ref, *refs):
    *far_refs, out_ref, done = refs
    count, _, block_rows, features = out_ref.shape
    copies = []

    def add(source, item, which, first, width):
        rows = pl.ds(pl.multiple_of(ids_ref[item, which] * block_rows, block_rows), block_rows)
        copies.append(
            pltpu.make_async_copy(
                source.at[rows, pl.ds(0, width)],
                out_ref.at[item, which, :, pl.ds(first, width)],
                done.at[len(copies)],
            )
        )

    for item in range(count):
        add(stored_ref, item, 0, 0, features)
        first = 0
        for far_ref in far_refs:
            add(far_ref, item, 1, first, far_ref.shape[1])
            first += far_ref.shape[1]
    run_copies(copies)


def pick_pairs(ids, passage_emb, far_parts, block_rows):
    count = ids.shape[0]
    features = sum(part.shape[1] for part in far_parts)
    return pl.pallas_call(
        pick_pairs_kernel,
        out_shape=pltpu.VMEM((count, 2, block_rows, features), passage_emb.dtype),
        in_specs=[IN_SMEM] + [IN_HBM] * (1 + len(far_parts)),
        out_specs=IN_VMEM,
        scratch_shapes=[pltpu.SemaphoreType.DMA((count * (1 + len(far_parts)),))],
        compiler_params=pltpu.CompilerParams(vmem_limit_bytes=VMEM_LIMIT),
        cost_estimate=pl.CostEstimate(flops=10**12, bytes_accessed=10**9, transcendentals=0),
        name="pick_pairs",
    )(ids, hbm(passage_emb), *[hbm(part) for part in far_parts])


def block_copies(table_ref, block, source_ref, listed_ref, first, done):
    list_len = table_ref.shape[1]
    features = source_ref.shape[2]
    return [
        pltpu.make_async_copy(
            source_ref.at[table_ref[block, j]],
            listed_ref.at[block * list_len + j, :, pl.ds(first, features)],
            done.at[block * list_len + j],
        )
        for j in range(list_len)
    ]


def block_scores(query_ref, listed_ref, block, list_len, first, features):
    block_rows = listed_ref.shape[1]
    listed = listed_ref[block * list_len : (block + 1) * list_len, :, first : first + features]
    return lax.dot_general(
        query_ref[block * block_rows : (block + 1) * block_rows, first : first + features],
        listed.reshape(list_len * block_rows, features),
        (((1,), (1,)), ((), ())),
        preferred_element_type=jnp.float32,
    )


def near_score_kernel(near_slots_ref, query_ref, near_ref, score_ref, listed_ref, done):
    query_blocks, list_len = near_slots_ref.shape
    copies = [
        block_copies(near_slots_ref, b, near_ref, listed_ref, 0, done)
        for b in range(query_blocks)
    ]
    for copy in sum(copies, []):
        copy.start()
    for b in range(query_blocks):
        for copy in copies[b]:
            copy.wait()
        score_ref[b] = block_scores(query_ref, listed_ref, b, list_len, 0, near_ref.shape[2])


def near_scores(near_slots, query_emb, near):
    query_blocks, list_len = near_slots.shape
    _, block_rows, features = near.shape
    columns = list_len * block_rows
    listed_count = query_blocks * list_len
    return pl.pallas_call(
        near_score_kernel,
        out_shape=jax.ShapeDtypeStruct((query_blocks, block_rows, columns), jnp.float32),
        in_specs=[IN_SMEM, IN_VMEM, IN_HBM],
        out_specs=IN_VMEM,
        scratch_shapes=[
            pltpu.VMEM((listed_count, block_rows, features), near.dtype),
            pltpu.SemaphoreType.DMA((listed_count,)),
        ],
        compiler_params=pltpu.CompilerParams(vmem_limit_bytes=VMEM_LIMIT),
        cost_estimate=pl.CostEstimate(
            flops=2 * query_blocks * block_rows * columns * features,
            bytes_accessed=2 * listed_count * block_rows * features + 2 * query_emb.size,
            transcendentals=0,
        ),
        name="near_scores",
    )(near_slots, query_emb, hbm(near))


def score_kernel(
    near_slots_ref, slots_ref, query_ref, positive_ref, before_ref, near_ref, fetched_ref, *refs
):
    score_ref, listed_ref, held_positive_ref, near_done, done = refs
    query_blocks, list_len = slots_ref.shape
    near_features, features = near_ref.shape[2], fetched_ref.shape[2]
    blocks = range(query_blocks)
    copies = [
        block_copies(slots_ref, b, fetched_ref, listed_ref, near_features, done) for b in blocks
    ]
    near_copies = [
        block_copies(near_slots_ref, b, near_ref, listed_ref, 0, near_done) for b in blocks
    ]
    for copy in sum(copies + near_copies, []):
        copy.start()
    held_positive_ref[...] = positive_ref[...]
    for b in blocks:
        for copy in copies[b]:
            copy.wait()
        score_ref[b] = before_ref[b] + block_scores(
            query_ref, listed_ref, b, list_len, near_features, features
        )
    for copy in sum(near_copies, []):
        copy.wait()


def partial_scores(near_slots, slots, query_emb, positive, before, near, fetched):
    query_blocks, list_len = slots.shape
    block_rows = fetched.shape[1]
    features = query_emb.shape[1]
    columns = list_len * block_rows
    listed_count = query_blocks * list_len
    return pl.pallas_call(
        score_kernel,
        out_shape=(
            pltpu.VMEM((query_blocks, block_rows, columns), jnp.float32),
            pltpu.VMEM((listed_count, block_rows, features), fetched.dtype),
            pltpu.VMEM((query_blocks, 1, block_rows), jnp.int32),
        ),
        in_specs=[IN_SMEM] * 2 + [IN_VMEM] * 3 + [IN_HBM] * 2,
        out_specs=[IN_VMEM] * 3,
        scratch_shapes=[pltpu.SemaphoreType.DMA((listed_count,))] * 2,
        compiler_params=pltpu.CompilerParams(vmem_limit_bytes=VMEM_LIMIT),
        cost_estimate=pl.CostEstimate(
            flops=2 * query_blocks * block_rows * columns * fetched.shape[2],
            bytes_accessed=2 * listed_count * block_rows * features + 2 * query_emb.size,
            transcendentals=0,
        ),
        name="partial_scores",
    )(
        near_slots,
        slots,
        query_emb,
        positive.reshape(query_blocks, 1, block_rows),
        before,
        hbm(near),
        hbm(fetched),
    )


def gradient_kernel(share_count, share_ref, *refs):
    score_refs = refs[:share_count]
    listed_ref, positive_ref, loss_ref, grad_ref = refs[share_count:]
    block = pl.program_id(0)
    block_rows, features = grad_ref.shape
    list_len = listed_ref.shape[0] // pl.num_programs(0)
    total = score_refs[0][block]
    for ref in score_refs[1:]:
        total = total + ref[block]
    scores = total * 50.0
    row_max = jnp.max(scores, axis=1, keepdims=True)
    log_total = row_max + jnp.log(jnp.sum(jnp.exp(scores - row_max), axis=1, keepdims=True))
    square = (block_rows, block_rows)
    positive = jnp.broadcast_to(positive_ref[block], square).T[:, :1]
    matched = lax.broadcasted_iota(jnp.int32, scores.shape, 1) == positive
    picked = jnp.sum(jnp.where(matched, scores, 0.0), axis=1, keepdims=True)
    losses = jnp.broadcast_to(log_total - picked, square).T[:1]
    held = loss_ref.shape[0]

    @pl.when(block // held == share_ref[0])
    def _():
        loss_ref[block % held] = losses

    weights = (jnp.exp(scores - log_total) - matched.astype(jnp.float32)).astype(jnp.bfloat16)
    tile = min(TILE, features)
    for f in range(0, features, tile):
        listed = listed_ref[pl.ds(block * list_len, list_len), :, f : f + tile]
        grad = jnp.dot(
            weights,
            listed.reshape(list_len * block_rows, tile),
            preferred_element_type=jnp.float32,
        )
        grad_ref[:, f : f + tile] = (grad * 50.0).astype(jnp.bfloat16)


def losses_and_gradients(share, share_blocks, scores, listed, positive):
    query_blocks, block_rows, columns = scores[0].shape
    features = listed.shape[2]
    rows = query_blocks * block_rows
    return pl.pallas_call(
        functools.partial(gradient_kernel, len(scores)),
        out_shape=(
            jax.ShapeDtypeStruct((share_blocks, 1, block_rows), jnp.float32),
            jax.ShapeDtypeStruct((rows, features), jnp.bfloat16),
        ),
        grid=(query_blocks,),
        in_specs=[IN_SMEM] + [IN_VMEM] * (len(scores) + 2),
        out_specs=[
            pl.BlockSpec((share_blocks, 1, block_rows), lambda b: (0, 0, 0)),
            pl.BlockSpec((block_rows, features), lambda b: (b, 0)),
        ],
        compiler_params=pltpu.CompilerParams(vmem_limit_bytes=VMEM_LIMIT),
        cost_estimate=pl.CostEstimate(
            flops=2 * rows * columns * features,
            bytes_accessed=2 * rows * features,
            transcendentals=2 * rows * columns,
        ),
        name="losses_and_gradients",
    )(share, *[vmem(score) for score in scores], vmem(listed), vmem(positive))


def shards(query_emb, passage_emb, cand_blocks, positive):
    dp_count = lax.axis_size("dp")
    fsdp_count = lax.axis_size("fsdp")
    query_blocks, list_len = cand_blocks.shape
    row_count, feature_count = query_emb.shape
    block_rows = row_count // query_blocks
    passage_blocks = passage_emb.shape[0] // block_rows
    half = dp_count // 2
    me = lax.axis_index("dp")
    me_in_half = me % half
    share = lax.axis_index("fsdp").astype(jnp.int32)
    cand_blocks, share = lax.optimization_barrier((cand_blocks, share))
    owners = cand_blocks // passage_blocks
    local_ids = cand_blocks % passage_blocks

    far = half + half // 2
    to_other_half = [(d, d ^ far) for d in range(dp_count)]
    first = LANES
    swapped = first + max(1, feature_count // LANES * 3 // 16) * LANES
    early_half = lax.ppermute(passage_emb[:, :first], "dp", to_other_half)

    quarter = dp_count // 4
    order = [quarter * z + c for c in range(quarter) for z in (0, 3, 1, 2)]
    places = jnp.asarray([order.index(d) for d in range(dp_count)], jnp.int32)

    def all_to_all(array):
        return lax.all_to_all(
            array, "dp", split_axis=0, concat_axis=0, tiled=True, axis_index_groups=[order]
        )

    member = jnp.asarray(order, jnp.int32)[:, None, None]
    both_ids = jnp.where(member == owners[None], local_ids[None], 0) + jnp.where(
        (member ^ far) == owners[None], SHIFT * local_ids[None], 0
    )
    requested = all_to_all(jnp.sum(both_ids, axis=(1, 2)).reshape(dp_count, 1)).reshape(dp_count)
    requested, early_half = lax.optimization_barrier((requested, early_half))
    late_half, requested = lax.optimization_barrier((passage_emb[:, first:swapped], requested))
    far_parts = [early_half, lax.ppermute(late_half, "dp", to_other_half)]
    picked = pick_blocks(requested % SHIFT, passage_emb, block_rows, swapped)
    fetched = all_to_all(picked)

    steps = jnp.arange(half, dtype=jnp.int32)
    readers = me - me_in_half + (me_in_half + steps) % half
    requested, far_parts[1] = lax.optimization_barrier((requested, far_parts[1]))
    relayed = requested[places[readers]]
    relayed = jnp.stack([relayed % SHIFT, relayed // SHIFT], axis=1)
    pairs = pick_pairs(relayed, passage_emb, far_parts, block_rows)
    near = jnp.concatenate(
        [pairs[0]]
        + [
            lax.ppermute(
                pairs[k],
                "dp",
                [(d, d - d % half + (d % half + k) % half) for d in range(dp_count)],
            )
            for k in range(1, half)
        ],
        axis=0,
    )
    is_far = (owners // half != me // half).astype(jnp.int32)
    near_slots = 2 * ((me - (owners ^ (far * is_far))) % half) + is_far
    near_slots = near_slots.astype(jnp.int32)

    before = near_scores(near_slots, query_emb, near)
    mine, listed, positive = partial_scores(
        near_slots, places[owners], query_emb, positive, before, near, fetched
    )
    scores = [mine] + [
        lax.ppermute(mine, "fsdp", [(i, (i + k) % fsdp_count) for i in range(fsdp_count)])
        for k in range(1, fsdp_count)
    ]
    share_rows = row_count // fsdp_count
    if share_rows % block_rows == 0:
        losses, query_grad = losses_and_gradients(
            share.reshape(1), share_rows // block_rows, scores, listed, positive
        )
        return losses.reshape(share_rows), query_grad
    whole = jnp.zeros((1,), jnp.int32)
    losses, query_grad = losses_and_gradients(whole, query_blocks, scores, listed, positive)
    losses = lax.dynamic_slice_in_dim(losses.reshape(row_count), share * share_rows, share_rows)
    return losses, query_grad


def solution(mesh):
    return jax.shard_map(
        shards,
        mesh=mesh,
        in_specs=(P("dp", "fsdp"), P("dp", "fsdp"), P("dp", None), P("dp")),
        out_specs=(P(("dp", "fsdp")), P("dp", "fsdp")),
        check_vma=False,
    )
```

```python
import functools

import jax
import jax.numpy as jnp
from jax import lax
from jax.experimental import pallas as pl
from jax.experimental.pallas import tpu as pltpu
from jax.sharding import PartitionSpec as P

VMEM_LIMIT = 32 * 1024 * 1024
TILE = 512
LANES = 128
WINDOW = 8
SHIFT = 1 << 16
IN_VMEM = pl.BlockSpec(memory_space=pltpu.VMEM)
IN_HBM = pl.BlockSpec(memory_space=pltpu.HBM)
IN_SMEM = pl.BlockSpec(memory_space=pltpu.SMEM)


def hbm(array):
    return pltpu.with_memory_space_constraint(array, pltpu.HBM)


def vmem(array):
    return pltpu.with_memory_space_constraint(array, pltpu.VMEM)


def run_copies(copies):
    for copy in copies:
        copy.start()
    for copy in copies:
        copy.wait()


def pick_kernel(ids_ref, stored_ref, out_ref, held_ref, loaded, done):
    count, block_rows, features = out_ref.shape
    first = stored_ref.shape[1] - features
    loads = [
        pltpu.make_async_copy(
            stored_ref.at[
                pl.ds(pl.multiple_of(ids_ref[i] * block_rows, block_rows), block_rows),
                pl.ds(first, features),
            ],
            held_ref.at[i],
            loaded.at[i],
        )
        for i in range(count)
    ]
    stores = [
        pltpu.make_async_copy(held_ref.at[i], out_ref.at[i], done.at[i]) for i in range(count)
    ]
    for load in loads[:WINDOW]:
        load.start()
    for i in range(count):
        loads[i].wait()
        stores[i].start()
        if i + WINDOW < count:
            loads[i + WINDOW].start()
    for store in stores:
        store.wait()


def pick_blocks(ids, passage_emb, block_rows, first):
    count, features = ids.shape[0], passage_emb.shape[1] - first
    return pl.pallas_call(
        pick_kernel,
        out_shape=pltpu.HBM((count, block_rows, features), passage_emb.dtype),
        in_specs=[IN_SMEM, IN_HBM],
        out_specs=IN_HBM,
        scratch_shapes=[
            pltpu.VMEM((count, block_rows, features), passage_emb.dtype),
            pltpu.SemaphoreType.DMA((count,)),
            pltpu.SemaphoreType.DMA((count,)),
        ],
        compiler_params=pltpu.CompilerParams(vmem_limit_bytes=VMEM_LIMIT),
        cost_estimate=pl.CostEstimate(
            flops=0, bytes_accessed=4 * count * block_rows * features, transcendentals=0
        ),
        name="pick_blocks",
    )(ids, hbm(passage_emb))


def pick_pairs_kernel(ids_ref, stored_ref, *refs):
    *far_refs, out_ref, done = refs
    count, _, block_rows, features = out_ref.shape
    copies = []

    def add(source, item, which, first, width):
        rows = pl.ds(pl.multiple_of(ids_ref[item, which] * block_rows, block_rows), block_rows)
        copies.append(
            pltpu.make_async_copy(
                source.at[rows, pl.ds(0, width)],
                out_ref.at[item, which, :, pl.ds(first, width)],
                done.at[len(copies)],
            )
        )

    for item in range(count):
        add(stored_ref, item, 0, 0, features)
        first = 0
        for far_ref in far_refs:
            add(far_ref, item, 1, first, far_ref.shape[1])
            first += far_ref.shape[1]
    run_copies(copies)


def pick_pairs(ids, passage_emb, far_parts, block_rows):
    count = ids.shape[0]
    features = sum(part.shape[1] for part in far_parts)
    return pl.pallas_call(
        pick_pairs_kernel,
        out_shape=pltpu.VMEM((count, 2, block_rows, features), passage_emb.dtype),
        in_specs=[IN_SMEM] + [IN_HBM] * (1 + len(far_parts)),
        out_specs=IN_VMEM,
        scratch_shapes=[pltpu.SemaphoreType.DMA((count * (1 + len(far_parts)),))],
        compiler_params=pltpu.CompilerParams(vmem_limit_bytes=VMEM_LIMIT),
        cost_estimate=pl.CostEstimate(flops=10**12, bytes_accessed=10**9, transcendentals=0),
        name="pick_pairs",
    )(ids, hbm(passage_emb), *[hbm(part) for part in far_parts])


def block_copies(table_ref, block, source_ref, listed_ref, first, done):
    list_len = table_ref.shape[1]
    features = source_ref.shape[2]
    return [
        pltpu.make_async_copy(
            source_ref.at[table_ref[block, j]],
            listed_ref.at[block * list_len + j, :, pl.ds(first, features)],
            done.at[block * list_len + j],
        )
        for j in range(list_len)
    ]


def block_scores(query_ref, listed_ref, block, list_len, first, features):
    block_rows = listed_ref.shape[1]
    listed = listed_ref[block * list_len : (block + 1) * list_len, :, first : first + features]
    return lax.dot_general(
        query_ref[block * block_rows : (block + 1) * block_rows, first : first + features],
        listed.reshape(list_len * block_rows, features),
        (((1,), (1,)), ((), ())),
        preferred_element_type=jnp.float32,
    )


def near_score_kernel(near_slots_ref, query_ref, near_ref, score_ref, listed_ref, done):
    query_blocks, list_len = near_slots_ref.shape
    copies = [
        block_copies(near_slots_ref, b, near_ref, listed_ref, 0, done)
        for b in range(query_blocks)
    ]
    for copy in sum(copies, []):
        copy.start()
    for b in range(query_blocks):
        for copy in copies[b]:
            copy.wait()
        score_ref[b] = block_scores(query_ref, listed_ref, b, list_len, 0, near_ref.shape[2])


def near_scores(near_slots, query_emb, near):
    query_blocks, list_len = near_slots.shape
    _, block_rows, features = near.shape
    columns = list_len * block_rows
    listed_count = query_blocks * list_len
    return pl.pallas_call(
        near_score_kernel,
        out_shape=jax.ShapeDtypeStruct((query_blocks, block_rows, columns), jnp.float32),
        in_specs=[IN_SMEM, IN_VMEM, IN_HBM],
        out_specs=IN_VMEM,
        scratch_shapes=[
            pltpu.VMEM((listed_count, block_rows, features), near.dtype),
            pltpu.SemaphoreType.DMA((listed_count,)),
        ],
        compiler_params=pltpu.CompilerParams(vmem_limit_bytes=VMEM_LIMIT),
        cost_estimate=pl.CostEstimate(
            flops=2 * query_blocks * block_rows * columns * features,
            bytes_accessed=2 * listed_count * block_rows * features + 2 * query_emb.size,
            transcendentals=0,
        ),
        name="near_scores",
    )(near_slots, query_emb, hbm(near))


def score_kernel(
    near_slots_ref, slots_ref, query_ref, positive_ref, before_ref, near_ref, fetched_ref, *refs
):
    score_ref, listed_ref, held_positive_ref, near_done, done = refs
    query_blocks, list_len = slots_ref.shape
    near_features, features = near_ref.shape[2], fetched_ref.shape[2]
    blocks = range(query_blocks)
    copies = [
        block_copies(slots_ref, b, fetched_ref, listed_ref, near_features, done) for b in blocks
    ]
    near_copies = [
        block_copies(near_slots_ref, b, near_ref, listed_ref, 0, near_done) for b in blocks
    ]
    for copy in sum(copies + near_copies, []):
        copy.start()
    held_positive_ref[...] = positive_ref[...]
    for b in blocks:
        for copy in copies[b]:
            copy.wait()
        score_ref[b] = before_ref[b] + block_scores(
            query_ref, listed_ref, b, list_len, near_features, features
        )
    for copy in sum(near_copies, []):
        copy.wait()


def partial_scores(near_slots, slots, query_emb, positive, before, near, fetched):
    query_blocks, list_len = slots.shape
    block_rows = fetched.shape[1]
    features = query_emb.shape[1]
    columns = list_len * block_rows
    listed_count = query_blocks * list_len
    return pl.pallas_call(
        score_kernel,
        out_shape=(
            pltpu.VMEM((query_blocks, block_rows, columns), jnp.float32),
            pltpu.VMEM((listed_count, block_rows, features), fetched.dtype),
            pltpu.VMEM((query_blocks, 1, block_rows), jnp.int32),
        ),
        in_specs=[IN_SMEM] * 2 + [IN_VMEM] * 3 + [IN_HBM] * 2,
        out_specs=[IN_VMEM] * 3,
        scratch_shapes=[pltpu.SemaphoreType.DMA((listed_count,))] * 2,
        compiler_params=pltpu.CompilerParams(vmem_limit_bytes=VMEM_LIMIT),
        cost_estimate=pl.CostEstimate(
            flops=2 * query_blocks * block_rows * columns * fetched.shape[2],
            bytes_accessed=2 * listed_count * block_rows * features + 2 * query_emb.size,
            transcendentals=0,
        ),
        name="partial_scores",
    )(
        near_slots,
        slots,
        query_emb,
        positive.reshape(query_blocks, 1, block_rows),
        before,
        hbm(near),
        hbm(fetched),
    )


def gradient_kernel(share_count, share_ref, *refs):
    score_refs = refs[:share_count]
    listed_ref, positive_ref, loss_ref, grad_ref = refs[share_count:]
    block = pl.program_id(0)
    block_rows, features = grad_ref.shape
    list_len = listed_ref.shape[0] // pl.num_programs(0)
    total = score_refs[0][block]
    for ref in score_refs[1:]:
        total = total + ref[block]
    scores = total * 50.0
    row_max = jnp.max(scores, axis=1, keepdims=True)
    log_total = row_max + jnp.log(jnp.sum(jnp.exp(scores - row_max), axis=1, keepdims=True))
    square = (block_rows, block_rows)
    positive = jnp.broadcast_to(positive_ref[block], square).T[:, :1]
    matched = lax.broadcasted_iota(jnp.int32, scores.shape, 1) == positive
    picked = jnp.sum(jnp.where(matched, scores, 0.0), axis=1, keepdims=True)
    losses = jnp.broadcast_to(log_total - picked, square).T[:1]
    held = loss_ref.shape[0]

    @pl.when(block // held == share_ref[0])
    def _():
        loss_ref[block % held] = losses

    weights = (jnp.exp(scores - log_total) - matched.astype(jnp.float32)).astype(jnp.bfloat16)
    tile = min(TILE, features)
    for f in range(0, features, tile):
        listed = listed_ref[pl.ds(block * list_len, list_len), :, f : f + tile]
        grad = jnp.dot(
            weights,
            listed.reshape(list_len * block_rows, tile),
            preferred_element_type=jnp.float32,
        )
        grad_ref[:, f : f + tile] = (grad * 50.0).astype(jnp.bfloat16)


def losses_and_gradients(share, share_blocks, scores, listed, positive):
    query_blocks, block_rows, columns = scores[0].shape
    features = listed.shape[2]
    rows = query_blocks * block_rows
    return pl.pallas_call(
        functools.partial(gradient_kernel, len(scores)),
        out_shape=(
            jax.ShapeDtypeStruct((share_blocks, 1, block_rows), jnp.float32),
            jax.ShapeDtypeStruct((rows, features), jnp.bfloat16),
        ),
        grid=(query_blocks,),
        in_specs=[IN_SMEM] + [IN_VMEM] * (len(scores) + 2),
        out_specs=[
            pl.BlockSpec((share_blocks, 1, block_rows), lambda b: (0, 0, 0)),
            pl.BlockSpec((block_rows, features), lambda b: (b, 0)),
        ],
        compiler_params=pltpu.CompilerParams(vmem_limit_bytes=VMEM_LIMIT),
        cost_estimate=pl.CostEstimate(
            flops=2 * rows * columns * features,
            bytes_accessed=2 * rows * features,
            transcendentals=2 * rows * columns,
        ),
        name="losses_and_gradients",
    )(share, *[vmem(score) for score in scores], vmem(listed), vmem(positive))


def shards(query_emb, passage_emb, cand_blocks, positive):
    dp_count = lax.axis_size("dp")
    fsdp_count = lax.axis_size("fsdp")
    query_blocks, list_len = cand_blocks.shape
    row_count, feature_count = query_emb.shape
    block_rows = row_count // query_blocks
    passage_blocks = passage_emb.shape[0] // block_rows
    half = dp_count // 2
    me = lax.axis_index("dp")
    me_in_half = me % half
    share = lax.axis_index("fsdp").astype(jnp.int32)
    cand_blocks, share = lax.optimization_barrier((cand_blocks, share))
    owners = cand_blocks // passage_blocks
    local_ids = cand_blocks % passage_blocks

    far = half + half // 2
    to_other_half = [(d, d ^ far) for d in range(dp_count)]
    first = LANES
    swapped = first + max(1, feature_count // LANES * 3 // 16) * LANES
    early_half = lax.ppermute(passage_emb[:, :first], "dp", to_other_half)

    quarter = dp_count // 4
    order = [quarter * z + c for c in range(quarter) for z in (0, 3, 1, 2)]
    places = jnp.asarray([order.index(d) for d in range(dp_count)], jnp.int32)

    def all_to_all(array):
        return lax.all_to_all(
            array, "dp", split_axis=0, concat_axis=0, tiled=True, axis_index_groups=[order]
        )

    member = jnp.asarray(order, jnp.int32)[:, None, None]
    both_ids = jnp.where(member == owners[None], local_ids[None], 0) + jnp.where(
        (member ^ far) == owners[None], SHIFT * local_ids[None], 0
    )
    requested = all_to_all(jnp.sum(both_ids, axis=(1, 2)).reshape(dp_count, 1)).reshape(dp_count)
    late_half, early_half = lax.optimization_barrier((passage_emb[:, first:swapped], early_half))
    far_parts = [early_half, lax.ppermute(late_half, "dp", to_other_half)]
    picked = pick_blocks(requested % SHIFT, passage_emb, block_rows, swapped)
    fetched = all_to_all(picked)

    steps = jnp.arange(half, dtype=jnp.int32)
    readers = me - me_in_half + (me_in_half + steps) % half
    requested, far_parts[1] = lax.optimization_barrier((requested, far_parts[1]))
    relayed = requested[places[readers]]
    relayed = jnp.stack([relayed % SHIFT, relayed // SHIFT], axis=1)
    pairs = pick_pairs(relayed, passage_emb, far_parts, block_rows)
    near = jnp.concatenate(
        [pairs[0]]
        + [
            lax.ppermute(
                pairs[k],
                "dp",
                [(d, d - d % half + (d % half + k) % half) for d in range(dp_count)],
            )
            for k in range(1, half)
        ],
        axis=0,
    )
    is_far = (owners // half != me // half).astype(jnp.int32)
    near_slots = 2 * ((me - (owners ^ (far * is_far))) % half) + is_far
    near_slots = near_slots.astype(jnp.int32)

    before = near_scores(near_slots, query_emb, near)
    mine, listed, positive = partial_scores(
        near_slots, places[owners], query_emb, positive, before, near, fetched
    )
    scores = [mine] + [
        lax.ppermute(mine, "fsdp", [(i, (i + k) % fsdp_count) for i in range(fsdp_count)])
        for k in range(1, fsdp_count)
    ]
    share_rows = row_count // fsdp_count
    if share_rows % block_rows == 0:
        losses, query_grad = losses_and_gradients(
            share.reshape(1), share_rows // block_rows, scores, listed, positive
        )
        return losses.reshape(share_rows), query_grad
    whole = jnp.zeros((1,), jnp.int32)
    losses, query_grad = losses_and_gradients(whole, query_blocks, scores, listed, positive)
    losses = lax.dynamic_slice_in_dim(losses.reshape(row_count), share * share_rows, share_rows)
    return losses, query_grad


def solution(mesh):
    return jax.shard_map(
        shards,
        mesh=mesh,
        in_specs=(P("dp", "fsdp"), P("dp", "fsdp"), P("dp", None), P("dp")),
        out_specs=(P(("dp", "fsdp")), P("dp", "fsdp")),
        check_vma=False,
    )
```

```python
import functools

import jax
import jax.numpy as jnp
from jax import lax
from jax.experimental import pallas as pl
from jax.experimental.pallas import tpu as pltpu
from jax.sharding import PartitionSpec as P

VMEM_LIMIT = 32 * 1024 * 1024
TILE = 512
LANES = 128
WINDOW = 8
SHIFT = 1 << 16
IN_VMEM = pl.BlockSpec(memory_space=pltpu.VMEM)
IN_HBM = pl.BlockSpec(memory_space=pltpu.HBM)
IN_SMEM = pl.BlockSpec(memory_space=pltpu.SMEM)


def hbm(array):
    return pltpu.with_memory_space_constraint(array, pltpu.HBM)


def vmem(array):
    return pltpu.with_memory_space_constraint(array, pltpu.VMEM)


def run_copies(copies):
    for copy in copies:
        copy.start()
    for copy in copies:
        copy.wait()


def pick_kernel(ids_ref, stored_ref, out_ref, held_ref, loaded, done):
    count, block_rows, features = out_ref.shape
    first = stored_ref.shape[1] - features
    loads = [
        pltpu.make_async_copy(
            stored_ref.at[
                pl.ds(pl.multiple_of(ids_ref[i] * block_rows, block_rows), block_rows),
                pl.ds(first, features),
            ],
            held_ref.at[i],
            loaded.at[i],
        )
        for i in range(count)
    ]
    stores = [
        pltpu.make_async_copy(held_ref.at[i], out_ref.at[i], done.at[i]) for i in range(count)
    ]
    for load in loads[:WINDOW]:
        load.start()
    for i in range(count):
        loads[i].wait()
        stores[i].start()
        if i + WINDOW < count:
            loads[i + WINDOW].start()
    for store in stores:
        store.wait()


def pick_blocks(ids, passage_emb, block_rows, first):
    count, features = ids.shape[0], passage_emb.shape[1] - first
    return pl.pallas_call(
        pick_kernel,
        out_shape=pltpu.HBM((count, block_rows, features), passage_emb.dtype),
        in_specs=[IN_SMEM, IN_HBM],
        out_specs=IN_HBM,
        scratch_shapes=[
            pltpu.VMEM((count, block_rows, features), passage_emb.dtype),
            pltpu.SemaphoreType.DMA((count,)),
            pltpu.SemaphoreType.DMA((count,)),
        ],
        compiler_params=pltpu.CompilerParams(vmem_limit_bytes=VMEM_LIMIT),
        cost_estimate=pl.CostEstimate(
            flops=0, bytes_accessed=4 * count * block_rows * features, transcendentals=0
        ),
        name="pick_blocks",
    )(ids, hbm(passage_emb))


def pick_pairs_kernel(ids_ref, stored_ref, *refs):
    *far_refs, out_ref, done = refs
    count, _, block_rows, features = out_ref.shape
    copies = []

    def add(source, item, which, first, width):
        rows = pl.ds(pl.multiple_of(ids_ref[item, which] * block_rows, block_rows), block_rows)
        copies.append(
            pltpu.make_async_copy(
                source.at[rows, pl.ds(0, width)],
                out_ref.at[item, which, :, pl.ds(first, width)],
                done.at[len(copies)],
            )
        )

    for item in range(count):
        add(stored_ref, item, 0, 0, features)
        first = 0
        for far_ref in far_refs:
            add(far_ref, item, 1, first, far_ref.shape[1])
            first += far_ref.shape[1]
    run_copies(copies)


def pick_pairs(ids, passage_emb, far_parts, block_rows):
    count = ids.shape[0]
    features = sum(part.shape[1] for part in far_parts)
    return pl.pallas_call(
        pick_pairs_kernel,
        out_shape=pltpu.VMEM((count, 2, block_rows, features), passage_emb.dtype),
        in_specs=[IN_SMEM] + [IN_HBM] * (1 + len(far_parts)),
        out_specs=IN_VMEM,
        scratch_shapes=[pltpu.SemaphoreType.DMA((count * (1 + len(far_parts)),))],
        compiler_params=pltpu.CompilerParams(vmem_limit_bytes=VMEM_LIMIT),
        cost_estimate=pl.CostEstimate(flops=10**11, bytes_accessed=10**9, transcendentals=0),
        name="pick_pairs",
    )(ids, hbm(passage_emb), *[hbm(part) for part in far_parts])


def block_copies(table_ref, block, source_ref, listed_ref, first, done):
    list_len = table_ref.shape[1]
    features = source_ref.shape[2]
    return [
        pltpu.make_async_copy(
            source_ref.at[table_ref[block, j]],
            listed_ref.at[block * list_len + j, :, pl.ds(first, features)],
            done.at[block * list_len + j],
        )
        for j in range(list_len)
    ]


def block_scores(query_ref, listed_ref, block, list_len, first, features):
    block_rows = listed_ref.shape[1]
    listed = listed_ref[block * list_len : (block + 1) * list_len, :, first : first + features]
    return lax.dot_general(
        query_ref[block * block_rows : (block + 1) * block_rows, first : first + features],
        listed.reshape(list_len * block_rows, features),
        (((1,), (1,)), ((), ())),
        preferred_element_type=jnp.float32,
    )


def near_score_kernel(near_slots_ref, query_ref, near_ref, score_ref, listed_ref, done):
    query_blocks, list_len = near_slots_ref.shape
    copies = [
        block_copies(near_slots_ref, b, near_ref, listed_ref, 0, done)
        for b in range(query_blocks)
    ]
    for copy in sum(copies, []):
        copy.start()
    for b in range(query_blocks):
        for copy in copies[b]:
            copy.wait()
        score_ref[b] = block_scores(query_ref, listed_ref, b, list_len, 0, near_ref.shape[2])


def near_scores(near_slots, query_emb, near):
    query_blocks, list_len = near_slots.shape
    _, block_rows, features = near.shape
    columns = list_len * block_rows
    listed_count = query_blocks * list_len
    return pl.pallas_call(
        near_score_kernel,
        out_shape=jax.ShapeDtypeStruct((query_blocks, block_rows, columns), jnp.float32),
        in_specs=[IN_SMEM, IN_VMEM, IN_HBM],
        out_specs=IN_VMEM,
        scratch_shapes=[
            pltpu.VMEM((listed_count, block_rows, features), near.dtype),
            pltpu.SemaphoreType.DMA((listed_count,)),
        ],
        compiler_params=pltpu.CompilerParams(vmem_limit_bytes=VMEM_LIMIT),
        cost_estimate=pl.CostEstimate(
            flops=2 * query_blocks * block_rows * columns * features,
            bytes_accessed=2 * listed_count * block_rows * features + 2 * query_emb.size,
            transcendentals=0,
        ),
        name="near_scores",
    )(near_slots, query_emb, hbm(near))


def score_kernel(
    near_slots_ref, slots_ref, query_ref, positive_ref, before_ref, near_ref, fetched_ref, *refs
):
    score_ref, listed_ref, held_positive_ref, near_done, done = refs
    query_blocks, list_len = slots_ref.shape
    near_features, features = near_ref.shape[2], fetched_ref.shape[2]
    blocks = range(query_blocks)
    copies = [
        block_copies(slots_ref, b, fetched_ref, listed_ref, near_features, done) for b in blocks
    ]
    near_copies = [
        block_copies(near_slots_ref, b, near_ref, listed_ref, 0, near_done) for b in blocks
    ]
    for copy in sum(copies + near_copies, []):
        copy.start()
    held_positive_ref[...] = positive_ref[...]
    for b in blocks:
        for copy in copies[b]:
            copy.wait()
        score_ref[b] = before_ref[b] + block_scores(
            query_ref, listed_ref, b, list_len, near_features, features
        )
    for copy in sum(near_copies, []):
        copy.wait()


def partial_scores(near_slots, slots, query_emb, positive, before, near, fetched):
    query_blocks, list_len = slots.shape
    block_rows = fetched.shape[1]
    features = query_emb.shape[1]
    columns = list_len * block_rows
    listed_count = query_blocks * list_len
    return pl.pallas_call(
        score_kernel,
        out_shape=(
            pltpu.VMEM((query_blocks, block_rows, columns), jnp.float32),
            pltpu.VMEM((listed_count, block_rows, features), fetched.dtype),
            pltpu.VMEM((query_blocks, 1, block_rows), jnp.int32),
        ),
        in_specs=[IN_SMEM] * 2 + [IN_VMEM] * 3 + [IN_HBM] * 2,
        out_specs=[IN_VMEM] * 3,
        scratch_shapes=[pltpu.SemaphoreType.DMA((listed_count,))] * 2,
        compiler_params=pltpu.CompilerParams(vmem_limit_bytes=VMEM_LIMIT),
        cost_estimate=pl.CostEstimate(
            flops=2 * query_blocks * block_rows * columns * fetched.shape[2],
            bytes_accessed=2 * listed_count * block_rows * features + 2 * query_emb.size,
            transcendentals=0,
        ),
        name="partial_scores",
    )(
        near_slots,
        slots,
        query_emb,
        positive.reshape(query_blocks, 1, block_rows),
        before,
        hbm(near),
        hbm(fetched),
    )


def gradient_kernel(share_count, share_ref, *refs):
    score_refs = refs[:share_count]
    listed_ref, positive_ref, loss_ref, grad_ref = refs[share_count:]
    block = pl.program_id(0)
    block_rows, features = grad_ref.shape
    list_len = listed_ref.shape[0] // pl.num_programs(0)
    total = score_refs[0][block]
    for ref in score_refs[1:]:
        total = total + ref[block]
    scores = total * 50.0
    row_max = jnp.max(scores, axis=1, keepdims=True)
    log_total = row_max + jnp.log(jnp.sum(jnp.exp(scores - row_max), axis=1, keepdims=True))
    square = (block_rows, block_rows)
    positive = jnp.broadcast_to(positive_ref[block], square).T[:, :1]
    matched = lax.broadcasted_iota(jnp.int32, scores.shape, 1) == positive
    picked = jnp.sum(jnp.where(matched, scores, 0.0), axis=1, keepdims=True)
    losses = jnp.broadcast_to(log_total - picked, square).T[:1]
    held = loss_ref.shape[0]

    @pl.when(block // held == share_ref[0])
    def _():
        loss_ref[block % held] = losses

    weights = (jnp.exp(scores - log_total) - matched.astype(jnp.float32)).astype(jnp.bfloat16)
    tile = min(TILE, features)
    for f in range(0, features, tile):
        listed = listed_ref[pl.ds(block * list_len, list_len), :, f : f + tile]
        grad = jnp.dot(
            weights,
            listed.reshape(list_len * block_rows, tile),
            preferred_element_type=jnp.float32,
        )
        grad_ref[:, f : f + tile] = (grad * 50.0).astype(jnp.bfloat16)


def losses_and_gradients(share, share_blocks, scores, listed, positive):
    query_blocks, block_rows, columns = scores[0].shape
    features = listed.shape[2]
    rows = query_blocks * block_rows
    return pl.pallas_call(
        functools.partial(gradient_kernel, len(scores)),
        out_shape=(
            jax.ShapeDtypeStruct((share_blocks, 1, block_rows), jnp.float32),
            jax.ShapeDtypeStruct((rows, features), jnp.bfloat16),
        ),
        grid=(query_blocks,),
        in_specs=[IN_SMEM] + [IN_VMEM] * (len(scores) + 2),
        out_specs=[
            pl.BlockSpec((share_blocks, 1, block_rows), lambda b: (0, 0, 0)),
            pl.BlockSpec((block_rows, features), lambda b: (b, 0)),
        ],
        compiler_params=pltpu.CompilerParams(vmem_limit_bytes=VMEM_LIMIT),
        cost_estimate=pl.CostEstimate(
            flops=2 * rows * columns * features,
            bytes_accessed=2 * rows * features,
            transcendentals=2 * rows * columns,
        ),
        name="losses_and_gradients",
    )(share, *[vmem(score) for score in scores], vmem(listed), vmem(positive))


def shards(query_emb, passage_emb, cand_blocks, positive):
    dp_count = lax.axis_size("dp")
    fsdp_count = lax.axis_size("fsdp")
    query_blocks, list_len = cand_blocks.shape
    row_count, feature_count = query_emb.shape
    block_rows = row_count // query_blocks
    passage_blocks = passage_emb.shape[0] // block_rows
    half = dp_count // 2
    me = lax.axis_index("dp")
    me_in_half = me % half
    share = lax.axis_index("fsdp").astype(jnp.int32)
    cand_blocks, share = lax.optimization_barrier((cand_blocks, share))
    owners = cand_blocks // passage_blocks
    local_ids = cand_blocks % passage_blocks

    far = half + half // 2
    to_other_half = [(d, d ^ far) for d in range(dp_count)]
    first = LANES
    swapped = first + max(1, feature_count // LANES * 3 // 16) * LANES
    early_half = lax.ppermute(passage_emb[:, :first], "dp", to_other_half)

    quarter = dp_count // 4
    columns = [*range(0, quarter, 2), *range(1, quarter, 2)]
    order = [quarter * z + c for c in columns for z in (0, 3, 1, 2)]
    places = jnp.asarray([order.index(d) for d in range(dp_count)], jnp.int32)

    def all_to_all(array):
        return lax.all_to_all(
            array, "dp", split_axis=0, concat_axis=0, tiled=True, axis_index_groups=[order]
        )

    member = jnp.asarray(order, jnp.int32)[:, None, None]
    both_ids = jnp.where(member == owners[None], local_ids[None], 0) + jnp.where(
        (member ^ far) == owners[None], SHIFT * local_ids[None], 0
    )
    requested = all_to_all(jnp.sum(both_ids, axis=(1, 2)).reshape(dp_count, 1)).reshape(dp_count)
    late_half, early_half = lax.optimization_barrier((passage_emb[:, first:swapped], early_half))
    far_parts = [early_half, lax.ppermute(late_half, "dp", to_other_half)]
    picked = pick_blocks(requested % SHIFT, passage_emb, block_rows, swapped)
    fetched = all_to_all(picked)

    steps = jnp.arange(half, dtype=jnp.int32)
    readers = me - me_in_half + (me_in_half + steps) % half
    requested, far_parts[1] = lax.optimization_barrier((requested, far_parts[1]))
    relayed = requested[places[readers]]
    relayed = jnp.stack([relayed % SHIFT, relayed // SHIFT], axis=1)
    pairs = pick_pairs(relayed, passage_emb, far_parts, block_rows)
    near = jnp.concatenate(
        [pairs[0]]
        + [
            lax.ppermute(
                pairs[k],
                "dp",
                [(d, d - d % half + (d % half + k) % half) for d in range(dp_count)],
            )
            for k in range(1, half)
        ],
        axis=0,
    )
    is_far = (owners // half != me // half).astype(jnp.int32)
    near_slots = 2 * ((me - (owners ^ (far * is_far))) % half) + is_far
    near_slots = near_slots.astype(jnp.int32)

    before = near_scores(near_slots, query_emb, near)
    mine, listed, positive = partial_scores(
        near_slots, places[owners], query_emb, positive, before, near, fetched
    )
    scores = [mine] + [
        lax.ppermute(mine, "fsdp", [(i, (i + k) % fsdp_count) for i in range(fsdp_count)])
        for k in range(1, fsdp_count)
    ]
    share_rows = row_count // fsdp_count
    if share_rows % block_rows == 0:
        losses, query_grad = losses_and_gradients(
            share.reshape(1), share_rows // block_rows, scores, listed, positive
        )
        return losses.reshape(share_rows), query_grad
    whole = jnp.zeros((1,), jnp.int32)
    losses, query_grad = losses_and_gradients(whole, query_blocks, scores, listed, positive)
    losses = lax.dynamic_slice_in_dim(losses.reshape(row_count), share * share_rows, share_rows)
    return losses, query_grad


def solution(mesh):
    return jax.shard_map(
        shards,
        mesh=mesh,
        in_specs=(P("dp", "fsdp"), P("dp", "fsdp"), P("dp", None), P("dp")),
        out_specs=(P(("dp", "fsdp")), P("dp", "fsdp")),
        check_vma=False,
    )
```

```python
import functools

import jax
import jax.numpy as jnp
from jax import lax
from jax.experimental import pallas as pl
from jax.experimental.pallas import tpu as pltpu
from jax.sharding import PartitionSpec as P

VMEM_LIMIT = 32 * 1024 * 1024
TILE = 1024
LANES = 128
WINDOW = 8
SHIFT = 1 << 16
IN_VMEM = pl.BlockSpec(memory_space=pltpu.VMEM)
IN_HBM = pl.BlockSpec(memory_space=pltpu.HBM)
IN_SMEM = pl.BlockSpec(memory_space=pltpu.SMEM)


def hbm(array):
    return pltpu.with_memory_space_constraint(array, pltpu.HBM)


def vmem(array):
    return pltpu.with_memory_space_constraint(array, pltpu.VMEM)


def run_copies(copies):
    for copy in copies:
        copy.start()
    for copy in copies:
        copy.wait()


def pick_kernel(ids_ref, stored_ref, out_ref, held_ref, loaded, done):
    count, block_rows, features = out_ref.shape
    first = stored_ref.shape[1] - features
    loads = [
        pltpu.make_async_copy(
            stored_ref.at[
                pl.ds(pl.multiple_of(ids_ref[i] * block_rows, block_rows), block_rows),
                pl.ds(first, features),
            ],
            held_ref.at[i],
            loaded.at[i],
        )
        for i in range(count)
    ]
    stores = [
        pltpu.make_async_copy(held_ref.at[i], out_ref.at[i], done.at[i]) for i in range(count)
    ]
    for load in loads[:WINDOW]:
        load.start()
    for i in range(count):
        loads[i].wait()
        stores[i].start()
        if i + WINDOW < count:
            loads[i + WINDOW].start()
    for store in stores:
        store.wait()


def pick_blocks(ids, passage_emb, block_rows, first):
    count, features = ids.shape[0], passage_emb.shape[1] - first
    return pl.pallas_call(
        pick_kernel,
        out_shape=pltpu.HBM((count, block_rows, features), passage_emb.dtype),
        in_specs=[IN_SMEM, IN_HBM],
        out_specs=IN_HBM,
        scratch_shapes=[
            pltpu.VMEM((count, block_rows, features), passage_emb.dtype),
            pltpu.SemaphoreType.DMA((count,)),
            pltpu.SemaphoreType.DMA((count,)),
        ],
        compiler_params=pltpu.CompilerParams(vmem_limit_bytes=VMEM_LIMIT),
        cost_estimate=pl.CostEstimate(
            flops=0, bytes_accessed=4 * count * block_rows * features, transcendentals=0
        ),
        name="pick_blocks",
    )(ids, hbm(passage_emb))


def pick_pairs_kernel(ids_ref, stored_ref, *refs):
    *far_refs, out_ref, done = refs
    count, _, block_rows, features = out_ref.shape
    copies = []

    def add(source, item, which, first, width):
        rows = pl.ds(pl.multiple_of(ids_ref[item, which] * block_rows, block_rows), block_rows)
        copies.append(
            pltpu.make_async_copy(
                source.at[rows, pl.ds(0, width)],
                out_ref.at[item, which, :, pl.ds(first, width)],
                done.at[len(copies)],
            )
        )

    for item in range(count):
        add(stored_ref, item, 0, 0, features)
        first = 0
        for far_ref in far_refs:
            add(far_ref, item, 1, first, far_ref.shape[1])
            first += far_ref.shape[1]
    run_copies(copies)


def pick_pairs(ids, passage_emb, far_parts, block_rows):
    count = ids.shape[0]
    features = sum(part.shape[1] for part in far_parts)
    return pl.pallas_call(
        pick_pairs_kernel,
        out_shape=pltpu.VMEM((count, 2, block_rows, features), passage_emb.dtype),
        in_specs=[IN_SMEM] + [IN_HBM] * (1 + len(far_parts)),
        out_specs=IN_VMEM,
        scratch_shapes=[pltpu.SemaphoreType.DMA((count * (1 + len(far_parts)),))],
        compiler_params=pltpu.CompilerParams(vmem_limit_bytes=VMEM_LIMIT),
        cost_estimate=pl.CostEstimate(flops=10**11, bytes_accessed=10**9, transcendentals=0),
        name="pick_pairs",
    )(ids, hbm(passage_emb), *[hbm(part) for part in far_parts])


def block_copies(table_ref, block, source_ref, listed_ref, first, done):
    list_len = table_ref.shape[1]
    features = source_ref.shape[2]
    return [
        pltpu.make_async_copy(
            source_ref.at[table_ref[block, j]],
            listed_ref.at[block * list_len + j, :, pl.ds(first, features)],
            done.at[block * list_len + j],
        )
        for j in range(list_len)
    ]


def block_scores(query_ref, listed_ref, block, list_len, first, features):
    block_rows = listed_ref.shape[1]
    listed = listed_ref[block * list_len : (block + 1) * list_len, :, first : first + features]
    return lax.dot_general(
        query_ref[block * block_rows : (block + 1) * block_rows, first : first + features],
        listed.reshape(list_len * block_rows, features),
        (((1,), (1,)), ((), ())),
        preferred_element_type=jnp.float32,
    )


def near_score_kernel(near_slots_ref, query_ref, near_ref, score_ref, listed_ref, done):
    query_blocks, list_len = near_slots_ref.shape
    copies = [
        block_copies(near_slots_ref, b, near_ref, listed_ref, 0, done)
        for b in range(query_blocks)
    ]
    for copy in sum(copies, []):
        copy.start()
    for b in range(query_blocks):
        for copy in copies[b]:
            copy.wait()
        score_ref[b] = block_scores(query_ref, listed_ref, b, list_len, 0, near_ref.shape[2])


def near_scores(near_slots, query_emb, near):
    query_blocks, list_len = near_slots.shape
    _, block_rows, features = near.shape
    columns = list_len * block_rows
    listed_count = query_blocks * list_len
    return pl.pallas_call(
        near_score_kernel,
        out_shape=jax.ShapeDtypeStruct((query_blocks, block_rows, columns), jnp.float32),
        in_specs=[IN_SMEM, IN_VMEM, IN_HBM],
        out_specs=IN_VMEM,
        scratch_shapes=[
            pltpu.VMEM((listed_count, block_rows, features), near.dtype),
            pltpu.SemaphoreType.DMA((listed_count,)),
        ],
        compiler_params=pltpu.CompilerParams(vmem_limit_bytes=VMEM_LIMIT),
        cost_estimate=pl.CostEstimate(
            flops=2 * query_blocks * block_rows * columns * features,
            bytes_accessed=2 * listed_count * block_rows * features + 2 * query_emb.size,
            transcendentals=0,
        ),
        name="near_scores",
    )(near_slots, query_emb, hbm(near))


def score_kernel(
    near_slots_ref, slots_ref, query_ref, positive_ref, before_ref, near_ref, fetched_ref, *refs
):
    score_ref, listed_ref, held_positive_ref, near_done, done = refs
    query_blocks, list_len = slots_ref.shape
    near_features, features = near_ref.shape[2], fetched_ref.shape[2]
    blocks = range(query_blocks)
    copies = [
        block_copies(slots_ref, b, fetched_ref, listed_ref, near_features, done) for b in blocks
    ]
    near_copies = [
        block_copies(near_slots_ref, b, near_ref, listed_ref, 0, near_done) for b in blocks
    ]
    for copy in sum(copies + near_copies, []):
        copy.start()
    held_positive_ref[...] = positive_ref[...]
    for b in blocks:
        for copy in copies[b]:
            copy.wait()
        score_ref[b] = before_ref[b] + block_scores(
            query_ref, listed_ref, b, list_len, near_features, features
        )
    for copy in sum(near_copies, []):
        copy.wait()


def partial_scores(near_slots, slots, query_emb, positive, before, near, fetched):
    query_blocks, list_len = slots.shape
    block_rows = fetched.shape[1]
    features = query_emb.shape[1]
    columns = list_len * block_rows
    listed_count = query_blocks * list_len
    return pl.pallas_call(
        score_kernel,
        out_shape=(
            pltpu.VMEM((query_blocks, block_rows, columns), jnp.float32),
            pltpu.VMEM((listed_count, block_rows, features), fetched.dtype),
            pltpu.VMEM((query_blocks, 1, block_rows), jnp.int32),
        ),
        in_specs=[IN_SMEM] * 2 + [IN_VMEM] * 3 + [IN_HBM] * 2,
        out_specs=[IN_VMEM] * 3,
        scratch_shapes=[pltpu.SemaphoreType.DMA((listed_count,))] * 2,
        compiler_params=pltpu.CompilerParams(vmem_limit_bytes=VMEM_LIMIT),
        cost_estimate=pl.CostEstimate(
            flops=2 * query_blocks * block_rows * columns * fetched.shape[2],
            bytes_accessed=2 * listed_count * block_rows * features + 2 * query_emb.size,
            transcendentals=0,
        ),
        name="partial_scores",
    )(
        near_slots,
        slots,
        query_emb,
        positive.reshape(query_blocks, 1, block_rows),
        before,
        hbm(near),
        hbm(fetched),
    )


def gradient_kernel(share_count, share_ref, *refs):
    score_refs = refs[:share_count]
    listed_ref, positive_ref, loss_ref, grad_ref = refs[share_count:]
    block = pl.program_id(0)
    block_rows, features = grad_ref.shape
    list_len = listed_ref.shape[0] // pl.num_programs(0)
    total = score_refs[0][block]
    for ref in score_refs[1:]:
        total = total + ref[block]
    scores = total * 50.0
    row_max = jnp.max(scores, axis=1, keepdims=True)
    log_total = row_max + jnp.log(jnp.sum(jnp.exp(scores - row_max), axis=1, keepdims=True))
    square = (block_rows, block_rows)
    positive = jnp.broadcast_to(positive_ref[block], square).T[:, :1]
    matched = lax.broadcasted_iota(jnp.int32, scores.shape, 1) == positive
    picked = jnp.sum(jnp.where(matched, scores, 0.0), axis=1, keepdims=True)
    losses = jnp.broadcast_to(log_total - picked, square).T[:1]
    held = loss_ref.shape[0]

    @pl.when(block // held == share_ref[0])
    def _():
        loss_ref[block % held] = losses

    weights = (jnp.exp(scores - log_total) - matched.astype(jnp.float32)).astype(jnp.bfloat16)
    tile = min(TILE, features)
    for f in range(0, features, tile):
        listed = listed_ref[pl.ds(block * list_len, list_len), :, f : f + tile]
        grad = jnp.dot(
            weights,
            listed.reshape(list_len * block_rows, tile),
            preferred_element_type=jnp.float32,
        )
        grad_ref[:, f : f + tile] = (grad * 50.0).astype(jnp.bfloat16)


def losses_and_gradients(share, share_blocks, scores, listed, positive):
    query_blocks, block_rows, columns = scores[0].shape
    features = listed.shape[2]
    rows = query_blocks * block_rows
    return pl.pallas_call(
        functools.partial(gradient_kernel, len(scores)),
        out_shape=(
            jax.ShapeDtypeStruct((share_blocks, 1, block_rows), jnp.float32),
            jax.ShapeDtypeStruct((rows, features), jnp.bfloat16),
        ),
        grid=(query_blocks,),
        in_specs=[IN_SMEM] + [IN_VMEM] * (len(scores) + 2),
        out_specs=[
            pl.BlockSpec((share_blocks, 1, block_rows), lambda b: (0, 0, 0)),
            pl.BlockSpec((block_rows, features), lambda b: (b, 0)),
        ],
        compiler_params=pltpu.CompilerParams(vmem_limit_bytes=VMEM_LIMIT),
        cost_estimate=pl.CostEstimate(
            flops=2 * rows * columns * features,
            bytes_accessed=2 * rows * features,
            transcendentals=2 * rows * columns,
        ),
        name="losses_and_gradients",
    )(share, *[vmem(score) for score in scores], vmem(listed), vmem(positive))


def shards(query_emb, passage_emb, cand_blocks, positive):
    dp_count = lax.axis_size("dp")
    fsdp_count = lax.axis_size("fsdp")
    query_blocks, list_len = cand_blocks.shape
    row_count, feature_count = query_emb.shape
    block_rows = row_count // query_blocks
    passage_blocks = passage_emb.shape[0] // block_rows
    half = dp_count // 2
    me = lax.axis_index("dp")
    me_in_half = me % half
    share = lax.axis_index("fsdp").astype(jnp.int32)
    cand_blocks, share = lax.optimization_barrier((cand_blocks, share))
    owners = cand_blocks // passage_blocks
    local_ids = cand_blocks % passage_blocks

    far = half + half // 2
    to_other_half = [(d, d ^ far) for d in range(dp_count)]
    first = LANES
    swapped = first + max(1, feature_count // LANES * 3 // 16) * LANES
    early_half = lax.ppermute(passage_emb[:, :first], "dp", to_other_half)

    quarter = dp_count // 4
    columns = [*range(0, quarter, 2), *range(1, quarter, 2)]
    order = [quarter * z + c for c in columns for z in (0, 3, 1, 2)]
    places = jnp.asarray([order.index(d) for d in range(dp_count)], jnp.int32)

    def all_to_all(array):
        return lax.all_to_all(
            array, "dp", split_axis=0, concat_axis=0, tiled=True, axis_index_groups=[order]
        )

    member = jnp.asarray(order, jnp.int32)[:, None, None]
    both_ids = jnp.where(member == owners[None], local_ids[None], 0) + jnp.where(
        (member ^ far) == owners[None], SHIFT * local_ids[None], 0
    )
    requested = all_to_all(jnp.sum(both_ids, axis=(1, 2)).reshape(dp_count, 1)).reshape(dp_count)
    late_half, early_half = lax.optimization_barrier((passage_emb[:, first:swapped], early_half))
    far_parts = [early_half, lax.ppermute(late_half, "dp", to_other_half)]
    picked = pick_blocks(requested % SHIFT, passage_emb, block_rows, swapped)
    fetched = all_to_all(picked)

    steps = jnp.arange(half, dtype=jnp.int32)
    readers = me - me_in_half + (me_in_half + steps) % half
    requested, far_parts[1] = lax.optimization_barrier((requested, far_parts[1]))
    relayed = requested[places[readers]]
    relayed = jnp.stack([relayed % SHIFT, relayed // SHIFT], axis=1)
    pairs = pick_pairs(relayed, passage_emb, far_parts, block_rows)
    near = jnp.concatenate(
        [pairs[0]]
        + [
            lax.ppermute(
                pairs[k],
                "dp",
                [(d, d - d % half + (d % half + k) % half) for d in range(dp_count)],
            )
            for k in range(1, half)
        ],
        axis=0,
    )
    is_far = (owners // half != me // half).astype(jnp.int32)
    near_slots = 2 * ((me - (owners ^ (far * is_far))) % half) + is_far
    near_slots = near_slots.astype(jnp.int32)

    before = near_scores(near_slots, query_emb, near)
    mine, listed, positive = partial_scores(
        near_slots, places[owners], query_emb, positive, before, near, fetched
    )
    scores = [mine] + [
        lax.ppermute(mine, "fsdp", [(i, (i + k) % fsdp_count) for i in range(fsdp_count)])
        for k in range(1, fsdp_count)
    ]
    share_rows = row_count // fsdp_count
    if share_rows % block_rows == 0:
        losses, query_grad = losses_and_gradients(
            share.reshape(1), share_rows // block_rows, scores, listed, positive
        )
        return losses.reshape(share_rows), query_grad
    whole = jnp.zeros((1,), jnp.int32)
    losses, query_grad = losses_and_gradients(whole, query_blocks, scores, listed, positive)
    losses = lax.dynamic_slice_in_dim(losses.reshape(row_count), share * share_rows, share_rows)
    return losses, query_grad


def solution(mesh):
    return jax.shard_map(
        shards,
        mesh=mesh,
        in_specs=(P("dp", "fsdp"), P("dp", "fsdp"), P("dp", None), P("dp")),
        out_specs=(P(("dp", "fsdp")), P("dp", "fsdp")),
        check_vma=False,
    )
```
